32 devices in a mesh: tx: 4 (over y, x), ty: 8 (over z, core).
Axes of the slice: x: 2, y: 2, z: 4, core: 2. Of those that a mesh axis runs over, the one named last changes fastest.
Arguments:
- members: bfloat16 [32, 32, 512, 128], P('tx', 'ty'), may hold values from -4 to 4
- mean_state: float32 [32, 32, 512], P('tx', 'ty'), may hold values from -6 to 6
- obs_pert: bfloat16 [32, 32, 128, 128], P('tx', 'ty'), may hold values from -1.5 to 1.5
- obs_rinv: bfloat16 [32, 32, 128], P('tx', 'ty'), may hold values from 0.25 to 2
- innovation: bfloat16 [32, 32, 128], P('tx', 'ty'), may hold values from -12 to 12
- obs_count: int32 [32, 32], P('tx', 'ty'), may hold values from 1 to 128, as said below
- neighbours: int32 [32, 32, 12], P('tx', 'ty'), may hold values from 0 to 24, as said below
- loc_weight: float32 [32, 32, 12], P('tx', 'ty'), may hold values from 0.1 to 1
Outputs:
- analysis: bfloat16 [32, 32, 512, 128], P('tx', 'ty')
The draws below stay inside these ranges and needn't reach their ends.
Inputs may be any that keep to these rules, and one draw needn't show every extreme that they name: `obs_count`: counts run from 1 to 128; 128 is reached on some blocks of every device. `neighbours`: the 12 codes of a group are distinct, each naming an offset (c // 5 - 2, c % 5 - 2) of at most two blocks per direction.
All inputs are finite; a program needn't handle non-finite values.
Results may differ from the reference program's by a relative error of at most 0.0049.
Values may be sent and summed in bfloat16 or wider, within the bound.
A program may use at most 128 MiB of HBM per device.

```python
import math
import jax
import jax.numpy as jnp
from jax import lax

K = 128
OBS_B = 128
NL = 12
NSI = 5
CL = 512
OBX = 32
OBY = 32


def draw_innovation(key, part):
    rows = jnp.arange(OBX, dtype=jnp.float32)[:, None, None] / max(OBX - 1, 1)
    cols = jnp.arange(OBY, dtype=jnp.float32)[None, :, None] / max(OBY - 1, 1)
    scale = 0.6 * (1.0 + rows + cols)
    values = scale * jax.random.normal(jax.random.fold_in(key, 12), (OBX, OBY, OBS_B), jnp.float32)
    return jnp.clip(values, -12.0, 12.0).astype(jnp.bfloat16)


def draw_obs_count(key, part):
    base = jax.random.randint(jax.random.fold_in(key, 21), (OBX, OBY), 1, OBS_B + 1)
    skewed = jnp.maximum(1, base * base // OBS_B)
    flat = jnp.arange(OBX * OBY, dtype=jnp.int32).reshape(OBX, OBY)
    return jnp.where(flat % 7 == 3, OBS_B, skewed).astype(jnp.int32)


def draw_neighbours(key, part):
    scores = jax.random.randint(jax.random.fold_in(key, 31), (OBX, OBY, 25), 0, 2 ** 20) * 32
    scores = scores + jnp.arange(25, dtype=jnp.int32)
    order = jnp.argsort(scores, axis=-1)
    return order[:, :, :NL].astype(jnp.int32)


def block_levels(key, dims, shards, smallest, high):
    factor_of = 1.0
    for axis_at, shards_of in shards:
        heights = jax.random.uniform(jax.random.fold_in(jax.random.fold_in(key, 6), axis_at), (shards_of,), jnp.float32, smallest / len(shards), high / len(shards))
        factor_of = factor_of * jnp.repeat(jnp.exp(heights), dims[axis_at] // shards_of).reshape((-1,) + (1,) * (len(dims) - 1 - axis_at))
    return factor_of


def normal_values(stream_key, shape, spread, reach, shards=(), kind=jnp.bfloat16):
    factor_of = block_levels(stream_key, shape, shards, -0.22, 0.18) if shards else 1.0
    array = jax.random.normal(stream_key, shape, jnp.float32) * spread * factor_of
    return jnp.minimum(jnp.maximum(array, -reach), reach).astype(kind)


def setup_inputs(seed: int = 0) -> dict:
    arg_keys = jax.random.split(jax.random.key(seed), 9)
    return {
        "members": normal_values(arg_keys[0], (OBX, OBY, CL, K), 0.5, 4.0, ((0, 4), (1, 8))),
        "mean_state": normal_values(arg_keys[1], (OBX, OBY, CL), 1.0, 6.0, ((0, 4), (1, 8)), jnp.float32),
        "obs_pert": normal_values(arg_keys[2], (OBX, OBY, OBS_B, K), 0.25, 1.5, ((0, 4), (1, 8))),
        "obs_rinv": jnp.clip(jnp.exp(math.log(2.0) - 2.0794415 * jax.random.uniform(arg_keys[3], (OBX, OBY, OBS_B), jnp.float32) ** block_levels(arg_keys[3], (OBX, OBY, OBS_B), ((0, 4), (1, 8)), -0.2, 0.2)), 0.25, 2.0).astype(jnp.bfloat16),
        "innovation": draw_innovation(jax.random.fold_in(arg_keys[8], 71), 0),
        "obs_count": draw_obs_count(jax.random.fold_in(arg_keys[8], 71), 0),
        "neighbours": draw_neighbours(jax.random.fold_in(arg_keys[8], 71), 0),
        "loc_weight": jnp.clip(0.1 + 0.9 * jax.random.uniform(arg_keys[7], (OBX, OBY, NL), jnp.float32) ** block_levels(arg_keys[7], (OBX, OBY, NL), ((0, 4), (1, 8)), -0.2, 0.2), 0.1, 1.0),
    }


def transform(cmat, vsum, rho):
    width = cmat.shape[-1]
    identity = jnp.eye(width, dtype=jnp.float32)
    matrix = cmat + (width - 1) / rho * identity
    cnorm = jnp.sqrt(lax.optimization_barrier(jnp.sum(matrix * matrix, axis=(1, 2))))[:, None, None]
    root_iter = matrix / cnorm
    inv_iter = jnp.broadcast_to(identity, matrix.shape)
    for sweep in range(NSI):
        update = 1.5 * identity - 0.5 * jnp.einsum('gkl,glm->gkm', inv_iter, root_iter, precision=lax.Precision.HIGHEST)
        root_iter = jnp.einsum('gkl,glm->gkm', root_iter, update, precision=lax.Precision.HIGHEST)
        inv_iter = jnp.einsum('gkl,glm->gkm', update, inv_iter, precision=lax.Precision.HIGHEST)
    covar = jnp.einsum('gkl,glm->gkm', inv_iter, inv_iter, precision=lax.Precision.HIGHEST) / cnorm
    wbar = jnp.einsum('gkl,gl->gk', covar, vsum, precision=lax.Precision.HIGHEST)
    return jnp.sqrt(jnp.float32(width - 1)) * inv_iter / jnp.sqrt(cnorm) + wbar[:, :, None]

def reference(members, mean_state, obs_pert, obs_rinv, innovation, obs_count, neighbours, loc_weight):
    width = obs_pert.shape[3]
    slots = jnp.arange(obs_pert.shape[2], dtype=jnp.int32)
    live_slot = slots[None, None, :] < obs_count[:, :, None]
    obs_weight = jnp.where(live_slot, obs_rinv.astype(jnp.float32), jnp.float32(0.0))
    innov_f = innovation.astype(jnp.float32)
    pert_f = obs_pert.astype(jnp.float32)
    first_sum = jnp.sum(obs_weight * innov_f * innov_f)
    second_sum = jnp.sum(live_slot.astype(jnp.float32) + obs_weight * lax.optimization_barrier(jnp.sum(pert_f * pert_f, axis=-1)) / (width - 1))
    rho = first_sum / second_sum
    scaled = (pert_f * obs_weight[..., None]).astype(jnp.bfloat16).astype(jnp.float32)
    grams = jnp.einsum('abok,abol->abkl', scaled, pert_f, precision=lax.Precision.HIGHEST)
    vectors = jnp.einsum('abok,abo->abk', scaled, innov_f, precision=lax.Precision.HIGHEST)
    column_ids = jnp.arange(OBY, dtype=jnp.int32)

    def group_row(row):
        codes = neighbours[row]
        row_ids = jnp.mod(row + codes // 5 - 2, OBX).astype(jnp.int32)
        col_ids = jnp.mod(column_ids[:, None] + codes % 5 - 2, OBY).astype(jnp.int32)
        picked = grams[row_ids, col_ids]
        picked_v = vectors[row_ids, col_ids]
        cmat = jnp.einsum('jn,jnkl->jkl', loc_weight[row], picked, precision=lax.Precision.HIGHEST)
        vsum = jnp.einsum('jn,jnk->jk', loc_weight[row], picked_v, precision=lax.Precision.HIGHEST)
        return transform(cmat, vsum, rho)
    weights = lax.map(group_row, jnp.arange(OBX, dtype=jnp.int32))

    def analyse_row(row):
        centre = weights[row]
        upper = weights[jnp.mod(row + 1, OBX)]
        lower = weights[jnp.mod(row - 1, OBX)]
        blended = (4.0 * centre + upper + lower + jnp.roll(centre, -1, axis=0) + jnp.roll(centre, 1, axis=0)) / 8.0
        blended = blended.astype(jnp.bfloat16).astype(jnp.float32)
        result = jnp.einsum('brk,bkm->brm', members[row].astype(jnp.float32), blended, precision=lax.Precision.HIGHEST)
        return (result + mean_state[row][:, :, None]).astype(jnp.bfloat16)
    return lax.map(analyse_row, jnp.arange(OBX, dtype=jnp.int32))
```

```python
import functools
import math

import jax
import jax.numpy as jnp
from jax import lax
from jax.experimental import pallas as pl
from jax.experimental.pallas import tpu as pltpu
from jax.sharding import PartitionSpec as P

MESH = pl.DeviceIdType.MESH
HALO = 2
F32 = jnp.float32
BF16 = jnp.bfloat16


def offsets(nx, ny):
    found = {(dx, 0) for dx in range(1, nx)} | {(0, dy) for dy in range(1, ny)}
    found |= {(dx % nx, dy % ny) for dx in (-1, 1) for dy in (-1, 1)}
    return sorted(found - {(0, 0)})


def product(left, right):
    s, a = left
    t, b = right
    cross = jnp.dot(a.astype(BF16), b.astype(BF16), preferred_element_type=F32)
    return s * t, cross + (s * b + t * a)


def two_sweeps(y):
    s = [product(v, v) for v in y]
    inner = [
        (0.0625 * q[0] - 0.5625 * v[0] + 1.6875, 0.0625 * q[1] - 0.5625 * v[1])
        for q, v in zip(s, y)
    ]
    h = [product(q, i) for q, i in zip(s, inner)]
    return [(p[0] - 2.4375 * v[0] + 2.25, p[1] - 2.4375 * v[1]) for p, v in zip(h, y)]


def analysis_weights(nx, ny, cnt, nb, lw, pert, rinv, innov, out,
                     grams, wts, wsend, htx, hty, st_own, st_x, st_sum, st_y,
                     g_send, g_recv, x_send, x_recv, y_send, y_recv, w_send, w_recv):
    na, nbk, slots, width = pert.shape
    listed = nb.shape[2]
    half = width // 2
    mx, my = lax.axis_index("tx"), lax.axis_index("ty")

    def at(dx, dy):
        return {"tx": lax.rem(mx + (dx % nx), nx), "ty": lax.rem(my + (dy % ny), ny)}

    barrier = pltpu.get_barrier_semaphore()
    partners = offsets(nx, ny)
    for dx, dy in partners:
        pl.semaphore_signal(barrier, inc=1, device_id=at(dx, dy), device_id_type=MESH)

    lane = lax.broadcasted_iota(jnp.int32, (1, slots), 1)
    eye = (lax.broadcasted_iota(jnp.int32, (width, width), 0)
           == lax.broadcasted_iota(jnp.int32, (width, width), 1))
    hrow = lax.broadcasted_iota(jnp.int32, (half, width), 0)
    hlane = lax.broadcasted_iota(jnp.int32, (half, width), 1)

    def gram_row(a, sums):
        first, second = sums
        for b in range(nbk):
            p = pert[a, b]
            live = lane < cnt[a, b]
            q = jnp.where(live, rinv[a, b:b + 1, :].astype(F32), 0.0)
            d = innov[a, b:b + 1, :].astype(F32)
            qd = q * d
            hi = qd.astype(BF16)
            lo = (qd - hi.astype(F32)).astype(BF16)
            scaled = (jnp.transpose(p.astype(F32)) * q).astype(BF16)
            sub = lax.broadcasted_iota(jnp.int32, (16, slots), 0)
            tail = jnp.where(sub == 0, hi.astype(F32), jnp.where(sub == 1, lo.astype(F32), 0.0))
            g = jnp.dot(scaled, p, preferred_element_type=F32)
            v = jnp.dot(tail.astype(BF16), p, preferred_element_type=F32)
            diag = jnp.sum(jnp.where(eye, g, 0.0), axis=0, keepdims=True)
            first = first + qd * d
            second = second + (jnp.where(live, 1.0, 0.0) + diag * (1.0 / (width - 1)))
            lower = pltpu.roll(g[half:], half, 1)
            packed = jnp.where(hrow <= hlane, g[:half], lower)
            vec = v[0:1] + v[1:2]
            vhi = vec.astype(BF16).astype(F32)
            subw = lax.broadcasted_iota(jnp.int32, (16, width), 0)
            extra = jnp.where(subw == 0, diag,
                              jnp.where(subw == 1, vhi, jnp.where(subw == 2, vec - vhi, 0.0)))
            grams[a + HALO, b + HALO, :half, :] = packed.astype(BF16)
            grams[a + HALO, b + HALO, half:, :] = extra.astype(BF16)
        return first, second

    def span(step, n):
        if step == 0:
            return pl.ds(HALO, n), pl.ds(HALO, n)
        if step == 1:
            return pl.ds(n, HALO), pl.ds(0, HALO)
        return pl.ds(HALO, HALO), pl.ds(n + HALO, HALO)

    def halo_copy(k, dx, dy):
        sa, da = span(dx, na)
        sb, db = span(dy, nbk)
        return pltpu.make_async_remote_copy(
            src_ref=grams.at[sa, sb], dst_ref=grams.at[da, db],
            send_sem=g_send.at[k], recv_sem=g_recv.at[k],
            device_id=at(dx, dy), device_id_type=MESH)

    early = [(1, 0), (-1, 0), (1, 1), (1, -1), (-1, 1), (-1, -1)]
    late = [(0, 1), (0, -1)]
    zero = jnp.zeros((1, slots), F32)
    sums = lax.fori_loop(
        0, 2 * HALO, lambda i, s: gram_row(i + (na - 2 * HALO) * (i // HALO), s), (zero, zero))
    pl.semaphore_wait(barrier, len(partners))
    copies = [halo_copy(k, dx, dy) for k, (dx, dy) in enumerate(early)]
    for c in copies:
        c.start()
    sums = lax.fori_loop(HALO, na - HALO, gram_row, sums)
    more = [halo_copy(len(early) + k, dx, dy) for k, (dx, dy) in enumerate(late)]
    for c in more:
        c.start()
    copies += more

    rows8 = lax.broadcasted_iota(jnp.int32, (8, slots), 0)
    st_own[...] = jnp.where(rows8 == 0, sums[0], jnp.where(rows8 == 1, sums[1], 0.0))
    xs = [pltpu.make_async_remote_copy(
        src_ref=st_own, dst_ref=st_x.at[k - 1], send_sem=x_send.at[k - 1],
        recv_sem=x_recv.at[k - 1], device_id=at(k, 0), device_id_type=MESH)
        for k in range(1, nx)]
    for c in xs:
        c.start()
    for c in xs:
        c.wait_recv()
    st_sum[...] = st_own[...] + jnp.sum(st_x[...], axis=0)
    ys = [pltpu.make_async_remote_copy(
        src_ref=st_sum, dst_ref=st_y.at[k - 1], send_sem=y_send.at[k - 1],
        recv_sem=y_recv.at[k - 1], device_id=at(0, k), device_id_type=MESH)
        for k in range(1, ny)]
    for c in ys:
        c.start()
    for c in ys:
        c.wait_recv()
    total = jnp.sum(st_sum[...] + jnp.sum(st_y[...], axis=0), axis=1, keepdims=True)
    inflation = (width - 1) * total[1:2] / total[0:1]
    for c in copies:
        c.wait_recv()

    def listed_sum(a, b):
        acc = None
        for j in range(listed):
            code = nb[a, b, j]
            down = lax.shift_right_logical(code * 13, 6)
            block = grams[a + down, b + (code - 5 * down)].astype(F32)
            term = lw[a, b, j] * block
            acc = term if acc is None else acc + term
        return acc

    def unpack(acc):
        c = acc[:half]
        diag = acc[half:half + 1]
        vec = acc[half + 1:half + 2] + acc[half + 2:half + 3]
        flipped = jnp.transpose(jnp.concatenate([c, c], axis=0))
        top = jnp.where(hrow <= hlane, c, flipped[:half])
        shifted = pltpu.roll(c, half, 1)
        column = hlane - half
        square = jnp.where(hrow > column, shifted, jnp.where(hrow == column, diag, flipped[:half]))
        bottom = jnp.where(column < 0, flipped[half:], square)
        return jnp.concatenate([top, bottom], axis=0), vec

    def transform(groups, send):
        pairs = [unpack(listed_sum(a, b)) for a, b in groups]
        vecs = [v for _, v in pairs]
        ms = [jnp.where(eye, m + inflation, m) for m, _ in pairs]
        inv = [lax.rsqrt(jnp.sum(jnp.sum(m * m, axis=0, keepdims=True), axis=1, keepdims=True))
               for m in ms]
        mid = [jnp.sum(jnp.sum(jnp.where(eye, m, 0.0), axis=0, keepdims=True), axis=1,
                       keepdims=True) * (1.0 / width) for m in ms]
        y = [(c * i, jnp.where(eye, m - c, m) * i) for m, i, c in zip(ms, inv, mid)]
        z2 = two_sweeps(y)
        t2 = [product(v, product(z, z)) for v, z in zip(y, z2)]
        w = two_sweeps(t2)
        z4 = [product(z, u) for z, u in zip(z2, w)]
        t4 = [product(t, product(u, u)) for t, u in zip(t2, w)]
        z5 = [product(z, (1.5 - 0.5 * t[0], -0.5 * t[1])) for z, t in zip(z4, t4)]
        for (a, b), (z, r), v, i in zip(groups, z5, vecs, inv):
            rb = r.astype(BF16)
            x = jnp.broadcast_to(v, (16, width))
            for _ in range(2):
                x = z * x + jnp.dot(x.astype(BF16), rb, preferred_element_type=F32)
            shift = jnp.transpose(jnp.broadcast_to(x[0:1] * i, (width, width)))
            scale = math.sqrt(width - 1) * jnp.sqrt(i)
            weight = scale * jnp.where(eye, r + z, r) + shift
            wts[a, b] = weight
            if send:
                wsend[a, b] = weight.astype(BF16)

    def w_copy(k, src, dst, dx, dy):
        return pltpu.make_async_remote_copy(
            src_ref=src, dst_ref=dst, send_sem=w_send.at[k], recv_sem=w_recv.at[k],
            device_id=at(dx, dy), device_id_type=MESH)

    @pl.loop(0, 2)
    def _(i):
        transform([(i * (na - 1), b) for b in range(nbk)], True)

    wx = [w_copy(0, wsend.at[na - 1], htx.at[0], 1, 0), w_copy(1, wsend.at[0], htx.at[1], -1, 0)]
    for c in wx:
        c.start()

    @pl.loop(0, (na - 2) // 2)
    def _(i):
        transform([(1 + 2 * i + k, b) for k in range(2) for b in (0, nbk - 1)], True)

    wy = [w_copy(2, wsend.at[:, nbk - 1], hty.at[0], 0, 1),
          w_copy(3, wsend.at[:, 0], hty.at[1], 0, -1)]
    for c in wy:
        c.start()

    @pl.loop(0, (na - 2) // 2)
    def _(i):
        transform([(1 + 2 * i + k, b) for k in range(2) for b in range(1, nbk - 1)], False)

    def blend(a, b, lower, upper):
        left = wts[a, b - 1] if b > 0 else hty[0, a].astype(F32)
        right = wts[a, b + 1] if b < nbk - 1 else hty[1, a].astype(F32)
        out[a, b] = ((4.0 * wts[a, b] + (upper + lower) + (left + right)) * 0.125).astype(BF16)

    @pl.loop(1, na - 1)
    def _(a):
        for b in range(1, nbk - 1):
            blend(a, b, wts[a - 1, b], wts[a + 1, b])

    for c in wx:
        c.wait_recv()
    for c in wy:
        c.wait_recv()

    @pl.loop(1, na - 1)
    def _(a):
        for b in (0, nbk - 1):
            blend(a, b, wts[a - 1, b], wts[a + 1, b])

    for b in range(nbk):
        blend(0, b, htx[0, b].astype(F32), wts[1, b])
        blend(na - 1, b, wts[na - 2, b], htx[1, b].astype(F32))
    for c in copies + xs + ys + wx + wy:
        c.wait_send()


def apply_weights(members, mean, blended, out):
    for b in range(members.shape[1]):
        base = jnp.transpose(jnp.broadcast_to(mean[0, b:b + 1, :], (8, mean.shape[2])))[:, 0:1]
        value = jnp.dot(members[0, b], blended[0, b], preferred_element_type=F32)
        out[0, b] = (value + base).astype(BF16)


def shards(nx, ny, members, mean_state, obs_pert, obs_rinv, innovation, obs_count, neighbours,
           loc_weight):
    na, nbk, slots, width = obs_pert.shape
    smem = pl.BlockSpec(memory_space=pltpu.SMEM)
    vmem = pl.BlockSpec(memory_space=pltpu.VMEM)
    dma = pltpu.SemaphoreType.DMA
    half = width // 2
    blended = pl.pallas_call(
        functools.partial(analysis_weights, nx, ny),
        out_shape=jax.ShapeDtypeStruct((na, nbk, width, width), BF16),
        in_specs=[smem] * 3 + [vmem] * 3,
        out_specs=vmem,
        scratch_shapes=[
            pltpu.VMEM((na + 2 * HALO, nbk + 2 * HALO, half + 16, width), BF16),
            pltpu.VMEM((na, nbk, width, width), F32),
            pltpu.VMEM((na, nbk, width, width), BF16),
            pltpu.VMEM((2, nbk, width, width), BF16),
            pltpu.VMEM((2, na, width, width), BF16),
            pltpu.VMEM((8, slots), F32),
            pltpu.VMEM((nx - 1, 8, slots), F32),
            pltpu.VMEM((8, slots), F32),
            pltpu.VMEM((ny - 1, 8, slots), F32),
            dma((8,)), dma((8,)),
            dma((nx - 1,)), dma((nx - 1,)),
            dma((ny - 1,)), dma((ny - 1,)),
            dma((4,)), dma((4,)),
        ],
        compiler_params=pltpu.CompilerParams(
            collective_id=0, has_side_effects=True, vmem_limit_bytes=40 * 1024 * 1024),
    )(obs_count, neighbours, loc_weight, obs_pert, obs_rinv, innovation)
    levels = members.shape[2]
    return pl.pallas_call(
        apply_weights,
        grid=(na,),
        out_shape=jax.ShapeDtypeStruct(members.shape, BF16),
        in_specs=[
            pl.BlockSpec((1, nbk, levels, width), lambda i: (i, 0, 0, 0)),
            pl.BlockSpec((1, nbk, levels), lambda i: (i, 0, 0)),
            pl.BlockSpec((1, nbk, width, width), lambda i: (i, 0, 0, 0)),
        ],
        out_specs=pl.BlockSpec((1, nbk, levels, width), lambda i: (i, 0, 0, 0)),
        compiler_params=pltpu.CompilerParams(vmem_limit_bytes=32 * 1024 * 1024),
    )(members, mean_state, blended)


def solution(mesh):
    nx, ny = mesh.shape["tx"], mesh.shape["ty"]
    return jax.shard_map(
        functools.partial(shards, nx, ny),
        mesh=mesh,
        in_specs=(
            P("tx", "ty", None, None),
            P("tx", "ty", None),
            P("tx", "ty", None, None),
            P("tx", "ty", None),
            P("tx", "ty", None),
            P("tx", "ty"),
            P("tx", "ty", None),
            P("tx", "ty", None),
        ),
        out_specs=P("tx", "ty", None, None),
        check_vma=False,
    )
```

```python
import functools
import math

import jax
import jax.numpy as jnp
from jax import lax
from jax.experimental import pallas as pl
from jax.experimental.pallas import tpu as pltpu
from jax.sharding import PartitionSpec as P

MESH = pl.DeviceIdType.MESH
HALO = 2
F32 = jnp.float32
BF16 = jnp.bfloat16


def offsets(nx, ny):
    found = {(dx, 0) for dx in range(1, nx)} | {(0, dy) for dy in range(1, ny)}
    found |= {(dx % nx, dy % ny) for dx in (-1, 1) for dy in (-1, 1)}
    return sorted(found - {(0, 0)})


def matmul(a, b):
    return jnp.dot(a.astype(BF16), b.astype(BF16), preferred_element_type=F32)


def square(x):
    s, a = x
    return s * s, matmul(a, a) + (2.0 * s) * a


def product(left, right):
    s, a = left
    t, b = right
    return s * t, matmul(a, b) + (s * b + t * a)


def two_sweeps(y):
    sq = [square(v) for v in y]
    inner = [q[1] - 9.0 * v[1] for q, v in zip(sq, y)]
    cross = [matmul(q[1], i) for q, i in zip(sq, inner)]
    out = []
    for c, q, v in zip(cross, sq, y):
        mid = q[0] - 9.0 * v[0] + 27.0
        out.append((q[0] * mid - 39.0 * v[0] + 36.0,
                    c + ((mid + q[0]) * q[1] - (9.0 * q[0] + 39.0) * v[1])))
    return out


def scaled_by(x, factor):
    return x[0] * factor, x[1] * factor


def analysis_weights(nx, ny, cnt_h, nb_h, lw_h, pert_h, rinv_h, innov_h, mean_h,
                     out_h, mean_th,
                     out, mean_t, cnt, nb, lw, pert, rinv, innov, mean,
                     grams, landed, wts, wsend, htx, hty, st_own, st_x, st_sum, st_y,
                     i_sem, p_sem, o_sem, g_send, g_recv, x_send, x_recv, y_send, y_recv,
                     w_send, w_recv):
    na, nbk, slots, width = pert.shape
    listed = nb.shape[2]
    half = width // 2
    mx, my = lax.axis_index("tx"), lax.axis_index("ty")

    def at(dx, dy):
        return {"tx": lax.rem(mx + (dx % nx), nx), "ty": lax.rem(my + (dy % ny), ny)}

    barrier = pltpu.get_barrier_semaphore()
    partners = offsets(nx, ny)
    for dx, dy in partners:
        pl.semaphore_signal(barrier, inc=1, device_id=at(dx, dy), device_id_type=MESH)

    def pair_at(i):
        h = i // 2
        return (1 - h) * (na - 2) * i + h * 2 * (i - 1)

    loads = [pltpu.make_async_copy(src, dst, i_sem.at[k]) for k, (src, dst) in enumerate([
        (cnt_h, cnt), (rinv_h, rinv), (innov_h, innov), (nb_h, nb), (lw_h, lw), (mean_h, mean)])]
    for c in loads[:3]:
        c.start()

    def pert_load(i):
        rows = pl.ds(pair_at(i), 2)
        return pltpu.make_async_copy(pert_h.at[rows], pert.at[rows], p_sem.at[i])

    for i in range(na // 2):
        pert_load(i).start()
    for c in loads[3:]:
        c.start()
    for c in loads[:3]:
        c.wait()

    lane = lax.broadcasted_iota(jnp.int32, (1, slots), 1)
    eye = (lax.broadcasted_iota(jnp.int32, (width, width), 0)
           == lax.broadcasted_iota(jnp.int32, (width, width), 1))
    hrow = lax.broadcasted_iota(jnp.int32, (half, width), 0)
    hlane = lax.broadcasted_iota(jnp.int32, (half, width), 1)
    sub = lax.broadcasted_iota(jnp.int32, (16, slots), 0)
    subw = lax.broadcasted_iota(jnp.int32, (16, width), 0)

    def gram_terms(a, b):
        p = pert[a, b]
        live = lane < cnt[b, a]
        q = jnp.where(live, rinv[a, b:b + 1, :].astype(F32), 0.0)
        d = innov[a, b:b + 1, :].astype(F32)
        qd = q * d
        hi = qd.astype(BF16).astype(F32)
        scaled = (jnp.transpose(p.astype(F32)) * q).astype(BF16)
        tail = jnp.where(sub == 0, hi, jnp.where(sub == 1, qd - hi, 0.0))
        g = jnp.dot(scaled, p, preferred_element_type=F32)
        v = jnp.dot(tail.astype(BF16), p, preferred_element_type=F32)
        diag = jnp.sum(jnp.where(eye, g, 0.0), axis=0, keepdims=True)
        lower = pltpu.roll(g[half:], half, 1)
        packed = jnp.where(hrow <= hlane, g[:half], lower)
        vec = v[0:1] + v[1:2]
        vhi = vec.astype(BF16).astype(F32)
        extra = jnp.where(subw == 0, diag,
                          jnp.where(subw == 1, vhi, jnp.where(subw == 2, vec - vhi, 0.0)))
        grams[a + HALO, b + HALO, :half, :] = packed.astype(BF16)
        grams[a + HALO, b + HALO, half:, :] = extra.astype(BF16)
        return qd * d, jnp.where(live, 1.0, 0.0) + diag * (1.0 / (width - 1))

    def span(step, n):
        if step == 0:
            return pl.ds(HALO, n), pl.ds(HALO, n)
        if step == 1:
            return pl.ds(n, HALO), pl.ds(0, HALO)
        return pl.ds(HALO, HALO), pl.ds(n + HALO, HALO)

    def halo_copy(k):
        dx, dy = directions[k]
        sa, da = span(dx, na)
        sb, db = span(dy, nbk)
        target = grams.at[da, db] if dx == 0 else landed.at[(1 - dx) // 2, :, db]
        return pltpu.make_async_remote_copy(
            src_ref=grams.at[sa, sb], dst_ref=target,
            send_sem=g_send.at[k], recv_sem=g_recv.at[k],
            device_id=at(dx, dy), device_id_type=MESH)

    directions = [(1, 0), (-1, 0), (0, 1), (0, -1), (1, 1), (1, -1), (-1, 1), (-1, -1)]

    def gram_rows(i, sums):
        first, second = sums
        pert_load(i).wait()
        base = pair_at(i)
        for k in range(2):
            for b in range(nbk):
                one, two = gram_terms(base + k, b)
                first, second = first + one, second + two

        @pl.when(i == 1)
        def _():
            pl.semaphore_wait(barrier, len(partners))
            for k in (0, 1):
                halo_copy(k).start()

        return first, second

    zero = jnp.zeros((1, slots), F32)
    sums = lax.fori_loop(0, na // 2, gram_rows, (zero, zero))
    rows8 = lax.broadcasted_iota(jnp.int32, (8, slots), 0)
    st_own[...] = jnp.where(rows8 == 0, sums[0], jnp.where(rows8 == 1, sums[1], 0.0))
    xs = [pltpu.make_async_remote_copy(
        src_ref=st_own, dst_ref=st_x.at[k - 1], send_sem=x_send.at[k - 1],
        recv_sem=x_recv.at[k - 1], device_id=at(k, 0), device_id_type=MESH)
        for k in range(1, nx)]
    for c in xs:
        c.start()
    for k in range(2, 8):
        halo_copy(k).start()

    loads[5].wait()

    @pl.loop(0, na)
    def _(a):
        row = mean[a]
        high = row.astype(BF16).astype(F32)
        rest = row - high
        middle = rest.astype(BF16).astype(F32)
        fill = jnp.zeros((width - 3 * nbk, row.shape[1]), F32)
        stack = jnp.concatenate([high, middle, rest - middle, fill], axis=0)
        mean_t[a] = jnp.transpose(stack).astype(BF16)

    mean_out = pltpu.make_async_copy(mean_t, mean_th, i_sem.at[6])
    mean_out.start()

    for c in xs:
        c.wait_recv()
    st_sum[...] = st_own[...] + jnp.sum(st_x[...], axis=0)
    ys = [pltpu.make_async_remote_copy(
        src_ref=st_sum, dst_ref=st_y.at[k - 1], send_sem=y_send.at[k - 1],
        recv_sem=y_recv.at[k - 1], device_id=at(0, k), device_id_type=MESH)
        for k in range(1, ny)]
    for c in ys:
        c.start()
    loads[3].wait()
    loads[4].wait()
    for c in ys:
        c.wait_recv()
    total = jnp.sum(st_sum[...] + jnp.sum(st_y[...], axis=0), axis=1, keepdims=True)
    inflation = (width - 1) * total[1:2] / total[0:1]
    for k in (2, 3):
        halo_copy(k).wait_recv()

    def listed_sum(a, b):
        acc = None
        for j in range(listed):
            code = nb[a, b, j]
            down = lax.shift_right_logical(code * 13, 6)
            block = grams[a + down, b + (code - 5 * down)].astype(F32)
            term = lw[a, b, j] * block
            acc = term if acc is None else acc + term
        return acc

    def unpack(acc):
        c = acc[:half]
        diag = acc[half:half + 1]
        vec = acc[half + 1:half + 2] + acc[half + 2:half + 3]
        flipped = jnp.transpose(jnp.concatenate([c, c], axis=0))
        top = jnp.where(hrow <= hlane, c, flipped[:half])
        shifted = pltpu.roll(c, half, 1)
        column = hlane - half
        corner = jnp.where(hrow > column, shifted, jnp.where(hrow == column, diag, flipped[:half]))
        bottom = jnp.where(column < 0, flipped[half:], corner)
        return jnp.concatenate([top, bottom], axis=0), vec

    def total_of(m):
        return jnp.sum(jnp.sum(m, axis=0, keepdims=True), axis=1, keepdims=True)

    def transform(groups):
        pairs = [unpack(listed_sum(a, b)) for a, b in groups]
        vecs = [v for _, v in pairs]
        ms = [jnp.where(eye, m + inflation, m) for m, _ in pairs]
        inv = [lax.rsqrt(total_of(m * m)) for m in ms]
        mid = [total_of(jnp.where(eye, m, 0.0)) * (1.0 / width) for m in ms]
        y = [(c * i, jnp.where(eye, m - c, m) * i) for m, i, c in zip(ms, inv, mid)]
        z2 = two_sweeps(y)
        v2 = [square(z) for z in z2]
        t2 = [scaled_by(product(p, v), 1.0 / 256) for p, v in zip(y, v2)]
        w = two_sweeps(t2)
        z4 = [product(z, u) for z, u in zip(z2, w)]
        v4 = [square(u) for u in w]
        t4 = [product(t, v) for t, v in zip(t2, v4)]
        z5 = [(z[0] * (768.0 - t[0]), (768.0 - t[0]) * z[1] - z[0] * t[1] - matmul(z[1], t[1]))
              for z, t in zip(z4, t4)]
        back = 1.0 / (256 * 512)
        z5 = [scaled_by(z, back) for z in z5]
        rb = [z[1].astype(BF16) for z in z5]
        x = [jnp.broadcast_to(v, (16, width)) for v in vecs]
        for _ in range(2):
            x = [z[0] * u + jnp.dot(u.astype(BF16), r, preferred_element_type=F32)
                 for z, u, r in zip(z5, x, rb)]
        shifts = [jnp.transpose(jnp.broadcast_to(u[0:1] * i, (width, width)))
                  for u, i in zip(x, inv)]
        for (a, b), (z, r), shift, i in zip(groups, z5, shifts, inv):
            scale = math.sqrt(width - 1) * jnp.sqrt(i)
            weight = scale * jnp.where(eye, r + z, r) + shift
            wts[a, b] = weight
            if b in (0, nbk - 1):
                wsend[a, b] = weight.astype(BF16)

    def w_copy(k, src, dst, dx, dy):
        return pltpu.make_async_remote_copy(
            src_ref=src, dst_ref=dst, send_sem=w_send.at[k], recv_sem=w_recv.at[k],
            device_id=at(dx, dy), device_id_type=MESH)

    def wx_copies():
        return [w_copy(0, wsend.at[na - 1], htx.at[0], 1, 0),
                w_copy(1, wsend.at[0], htx.at[1], -1, 0)]

    def wy_copies(k, first, count):
        rows = pl.ds(first, count)
        return [w_copy(k, wsend.at[rows, nbk - 1], hty.at[0, rows], 0, 1),
                w_copy(k + 1, wsend.at[rows, 0], hty.at[1, rows], 0, -1)]

    inner_wy = wy_copies(2, 2, na - 4)
    edge_wy = wy_copies(4, 0, 1) + wy_copies(6, na - 1, 1)
    last_wy = wy_copies(8, 1, 1) + wy_copies(10, na - 2, 1)
    inner = (na - 4) // 2

    @pl.loop(0, inner + 2)
    def _(i):
        h = i // inner
        r = i - inner * h

        @pl.when(i == inner)
        def _():
            for c in inner_wy:
                c.start()
            for k in (0, 1, 4, 5, 6, 7):
                halo_copy(k).wait_recv()
            for k in range(HALO):
                for b in range(nbk + 2 * HALO):
                    grams[k, b] = landed[0, k, b]
                    grams[na + HALO + k, b] = landed[1, k, b]

        one = (1 - h) * (2 + 2 * r) + h * r
        two = (1 - h) * (3 + 2 * r) + h * (na - 1 - r)
        transform([(a, b) for a in (one, two) for b in range(nbk)])
        for b in range(1, nbk - 1):
            for a in (one, two):
                wsend[a, b] = wts[a, b].astype(BF16)

        @pl.when(i == inner)
        def _():
            for c in wx_copies() + edge_wy:
                c.start()

    for c in last_wy:
        c.start()

    def blend(a, b, lower, upper):
        left = wts[a, b - 1] if b > 0 else hty[0, a].astype(F32)
        right = wts[a, b + 1] if b < nbk - 1 else hty[1, a].astype(F32)
        out[a, b] = ((4.0 * wts[a, b] + (upper + lower) + (left + right)) * 0.125).astype(BF16)

    @pl.loop(1, na - 1)
    def _(a):
        for b in range(1, nbk - 1):
            blend(a, b, wts[a - 1, b], wts[a + 1, b])

    for c in wx_copies() + inner_wy + edge_wy:
        c.wait_recv()
    for b in range(1, nbk - 1):
        blend(0, b, htx[0, b].astype(F32), wts[1, b])
        blend(na - 1, b, wts[na - 2, b], htx[1, b].astype(F32))
    for c in last_wy:
        c.wait_recv()

    def row_out(a):
        return pltpu.make_async_copy(out.at[a], out_h.at[a], o_sem.at[a])

    for b in (0, nbk - 1):
        blend(0, b, htx[0, b].astype(F32), wts[1, b])
        blend(na - 1, b, wts[na - 2, b], htx[1, b].astype(F32))
    row_out(0).start()
    row_out(na - 1).start()

    @pl.loop(1, na - 1)
    def _(a):
        for b in (0, nbk - 1):
            blend(a, b, wts[a - 1, b], wts[a + 1, b])
        row_out(a).start()

    for k in range(8):
        halo_copy(k).wait_send()
    for c in xs + ys + wx_copies() + inner_wy + edge_wy + last_wy:
        c.wait_send()
    mean_out.wait()
    for a in range(na):
        row_out(a).wait()


def apply_weights(members_h, mean_th, blended_h, out_h, members, mean_t, blended, result, sem):
    na, nbk, levels, width = members.shape
    row = lax.broadcasted_iota(jnp.int32, (width, width), 0)

    def loads(a):
        return [pltpu.make_async_copy(src.at[a], dst.at[a], sem.at[k, a])
                for k, (src, dst) in enumerate(
                    [(blended_h, blended), (mean_th, mean_t), (members_h, members)])]

    def copy_out(a):
        return pltpu.make_async_copy(result.at[a], out_h.at[a], sem.at[3, a])

    for a in range(na):
        for c in loads(a):
            c.start()

    @pl.loop(0, na)
    def _(a):
        for c in loads(a):
            c.wait()
        for b in range(nbk):
            pick = jnp.where((row == b) | (row == b + nbk) | (row == b + 2 * nbk), 1.0, 0.0)
            left = jnp.concatenate([members[a, b], mean_t[a]], axis=1)
            right = jnp.concatenate([blended[a, b], pick.astype(BF16)], axis=0)
            result[a, b] = jnp.dot(left, right, preferred_element_type=F32).astype(BF16)
        copy_out(a).start()

    @pl.loop(0, na)
    def _(a):
        copy_out(a).wait()


def shards(nx, ny, members, mean_state, obs_pert, obs_rinv, innovation, obs_count, neighbours,
           loc_weight):
    na, nbk, slots, width = obs_pert.shape
    levels = members.shape[2]
    hbm = pl.BlockSpec(memory_space=pltpu.HBM)
    dma = pltpu.SemaphoreType.DMA
    half = width // 2
    blended, mean_t = pl.pallas_call(
        functools.partial(analysis_weights, nx, ny),
        out_shape=[
            jax.ShapeDtypeStruct((na, nbk, width, width), BF16),
            jax.ShapeDtypeStruct((na, levels, width), BF16),
        ],
        in_specs=[hbm] * 7,
        out_specs=[hbm] * 2,
        scratch_shapes=[
            pltpu.VMEM((na, nbk, width, width), BF16),
            pltpu.VMEM((na, levels, width), BF16),
            pltpu.SMEM((nbk, na), jnp.int32),
            pltpu.SMEM(neighbours.shape, jnp.int32),
            pltpu.SMEM(loc_weight.shape, F32),
            pltpu.VMEM(obs_pert.shape, BF16),
            pltpu.VMEM(obs_rinv.shape, BF16),
            pltpu.VMEM(innovation.shape, BF16),
            pltpu.VMEM(mean_state.shape, F32),
            pltpu.VMEM((na + 2 * HALO, nbk + 2 * HALO, half + 16, width), BF16),
            pltpu.VMEM((2, HALO, nbk + 2 * HALO, half + 16, width), BF16),
            pltpu.VMEM((na, nbk, width, width), F32),
            pltpu.VMEM((na, nbk, width, width), BF16),
            pltpu.VMEM((2, nbk, width, width), BF16),
            pltpu.VMEM((2, na, width, width), BF16),
            pltpu.VMEM((8, slots), F32),
            pltpu.VMEM((nx - 1, 8, slots), F32),
            pltpu.VMEM((8, slots), F32),
            pltpu.VMEM((ny - 1, 8, slots), F32),
            dma((7,)), dma((na // 2,)), dma((na,)),
            dma((8,)), dma((8,)),
            dma((nx - 1,)), dma((nx - 1,)),
            dma((ny - 1,)), dma((ny - 1,)),
            dma((12,)), dma((12,)),
        ],
        compiler_params=pltpu.CompilerParams(
            collective_id=0, has_side_effects=True, vmem_limit_bytes=57 * 1024 * 1024),
    )(obs_count.T, neighbours, loc_weight, obs_pert, obs_rinv, innovation, mean_state)
    return pl.pallas_call(
        apply_weights,
        out_shape=jax.ShapeDtypeStruct(members.shape, BF16),
        in_specs=[hbm] * 3,
        out_specs=hbm,
        scratch_shapes=[
            pltpu.VMEM(members.shape, BF16),
            pltpu.VMEM((na, levels, width), BF16),
            pltpu.VMEM((na, nbk, width, width), BF16),
            pltpu.VMEM(members.shape, BF16),
            dma((4, na)),
        ],
        compiler_params=pltpu.CompilerParams(vmem_limit_bytes=57 * 1024 * 1024),
    )(members, mean_t, blended)


def solution(mesh):
    nx, ny = mesh.shape["tx"], mesh.shape["ty"]
    return jax.shard_map(
        functools.partial(shards, nx, ny),
        mesh=mesh,
        in_specs=(
            P("tx", "ty", None, None),
            P("tx", "ty", None),
            P("tx", "ty", None, None),
            P("tx", "ty", None),
            P("tx", "ty", None),
            P("tx", "ty"),
            P("tx", "ty", None),
            P("tx", "ty", None),
        ),
        out_specs=P("tx", "ty", None, None),
        check_vma=False,
    )
```

```python
import functools
import math

import jax
import jax.numpy as jnp
from jax import lax
from jax.experimental import pallas as pl
from jax.experimental.pallas import tpu as pltpu
from jax.sharding import PartitionSpec as P

MESH = pl.DeviceIdType.MESH
HALO = 2
F32 = jnp.float32
BF16 = jnp.bfloat16


def offsets(nx, ny):
    return [(dx, 0) for dx in range(1, nx)] + [(0, dy) for dy in range(1, ny)]


def matmul(a, b):
    return jnp.dot(a.astype(BF16), b.astype(BF16), preferred_element_type=F32)


def square(x):
    s, a = x
    return s * s, matmul(a, a) + (2.0 * s) * a


def product(left, right):
    s, a = left
    t, b = right
    return s * t, matmul(a, b) + (s * b + t * a)


def two_sweeps(y):
    sq = [square(v) for v in y]
    inner = [q[1] - 9.0 * v[1] for q, v in zip(sq, y)]
    cross = [matmul(q[1], i) for q, i in zip(sq, inner)]
    out = []
    for c, q, v in zip(cross, sq, y):
        mid = q[0] - 9.0 * v[0] + 27.0
        out.append((q[0] * mid - 39.0 * v[0] + 36.0,
                    c + ((mid + q[0]) * q[1] - (9.0 * q[0] + 39.0) * v[1])))
    return out


def scaled_by(x, factor):
    return x[0] * factor, x[1] * factor


def analysis_weights(nx, ny, cnt_h, nb_h, lw_h, pert_h, rinv_h, innov_h, mean_h,
                     out_h, mean_th,
                     out, mean_t, cnt, nb, lw, pert, rinv, innov, mean,
                     grams, landed, wts, wsend, htx, hty, st_own, st_x, st_sum, st_y,
                     i_sem, p_sem, o_sem, g_send, g_recv, x_send, x_recv, y_send, y_recv,
                     w_send, w_recv):
    na, nbk, slots, width = pert.shape
    listed = nb.shape[2]
    half = width // 2
    mx, my = lax.axis_index("tx"), lax.axis_index("ty")

    def at(dx, dy):
        return {"tx": lax.rem(mx + (dx % nx), nx), "ty": lax.rem(my + (dy % ny), ny)}

    barrier = pltpu.get_barrier_semaphore()
    partners = offsets(nx, ny)
    for dx, dy in partners:
        pl.semaphore_signal(barrier, inc=1, device_id=at(dx, dy), device_id_type=MESH)

    def pair_at(i):
        h = i // 2
        return (1 - h) * (na - 2) * i + h * 2 * (i - 1)

    loads = [pltpu.make_async_copy(src, dst, i_sem.at[k]) for k, (src, dst) in enumerate([
        (cnt_h, cnt), (rinv_h, rinv), (innov_h, innov), (nb_h, nb), (lw_h, lw), (mean_h, mean)])]
    for c in loads[:3]:
        c.start()

    def pert_load(i):
        rows = pl.ds(pair_at(i), 2)
        return pltpu.make_async_copy(pert_h.at[rows], pert.at[rows], p_sem.at[i])

    for i in range(na // 2):
        pert_load(i).start()
    for c in loads[3:]:
        c.start()
    for c in loads[:3]:
        c.wait()

    lane = lax.broadcasted_iota(jnp.int32, (1, slots), 1)
    eye = (lax.broadcasted_iota(jnp.int32, (width, width), 0)
           == lax.broadcasted_iota(jnp.int32, (width, width), 1))
    hrow = lax.broadcasted_iota(jnp.int32, (half, width), 0)
    hlane = lax.broadcasted_iota(jnp.int32, (half, width), 1)
    sub = lax.broadcasted_iota(jnp.int32, (16, slots), 0)
    subw = lax.broadcasted_iota(jnp.int32, (16, width), 0)

    def gram_terms(a, b):
        p = pert[a, b]
        live = lane < cnt[b, a]
        q = jnp.where(live, rinv[a, b:b + 1, :].astype(F32), 0.0)
        d = innov[a, b:b + 1, :].astype(F32)
        qd = q * d
        hi = qd.astype(BF16).astype(F32)
        scaled = (jnp.transpose(p.astype(F32)) * q).astype(BF16)
        tail = jnp.where(sub == 0, hi, jnp.where(sub == 1, qd - hi, 0.0))
        g = jnp.dot(scaled, p, preferred_element_type=F32)
        v = jnp.dot(tail.astype(BF16), p, preferred_element_type=F32)
        diag = jnp.sum(jnp.where(eye, g, 0.0), axis=0, keepdims=True)
        lower = pltpu.roll(g[half:], half, 1)
        packed = jnp.where(hrow <= hlane, g[:half], lower)
        vec = v[0:1] + v[1:2]
        vhi = vec.astype(BF16).astype(F32)
        extra = jnp.where(subw == 0, diag,
                          jnp.where(subw == 1, vhi, jnp.where(subw == 2, vec - vhi, 0.0)))
        grams[a + HALO, b + HALO, :half, :] = packed.astype(BF16)
        grams[a + HALO, b + HALO, half:, :] = extra.astype(BF16)
        return qd * d, jnp.where(live, 1.0, 0.0) + diag * (1.0 / (width - 1))

    def remote(src, dst, k, dx, dy):
        return pltpu.make_async_remote_copy(
            src_ref=src, dst_ref=dst, send_sem=g_send.at[k], recv_sem=g_recv.at[k],
            device_id=at(dx, dy), device_id_type=MESH)

    own_cols = pl.ds(HALO, nbk)
    ends = (pl.ds(0, HALO), pl.ds(nbk + HALO, HALO))

    def tx_copies(cols, k):
        return [remote(grams.at[pl.ds(na, HALO), cols], landed.at[0, :, cols], k, 1, 0),
                remote(grams.at[pl.ds(HALO, HALO), cols], landed.at[1, :, cols], k + 1, -1, 0)]

    def ty_copies(i):
        rows = pl.ds(HALO + pair_at(i), 2)
        k = 6 + 2 * i
        return [remote(grams.at[rows, pl.ds(nbk, HALO)], grams.at[rows, ends[0]], k, 0, 1),
                remote(grams.at[rows, pl.ds(HALO, HALO)], grams.at[rows, ends[1]], k + 1, 0, -1)]

    def corner_copies():
        return tx_copies(ends[0], 2) + tx_copies(ends[1], 4)

    def gram_rows(i, sums):
        first, second = sums
        pert_load(i).wait()
        base = pair_at(i)
        for k in range(2):
            for b in range(nbk):
                one, two = gram_terms(base + k, b)
                first, second = first + one, second + two

        @pl.when(i == 0)
        def _():
            pl.semaphore_wait(barrier, len(partners))

        for c in ty_copies(i):
            c.start()

        @pl.when(i == 1)
        def _():
            for c in tx_copies(own_cols, 0):
                c.start()

        return first, second

    zero = jnp.zeros((1, slots), F32)
    sums = lax.fori_loop(0, na // 2, gram_rows, (zero, zero))
    rows8 = lax.broadcasted_iota(jnp.int32, (8, slots), 0)
    st_own[...] = jnp.where(rows8 == 0, sums[0], jnp.where(rows8 == 1, sums[1], 0.0))
    xs = [pltpu.make_async_remote_copy(
        src_ref=st_own, dst_ref=st_x.at[k - 1], send_sem=x_send.at[k - 1],
        recv_sem=x_recv.at[k - 1], device_id=at(k, 0), device_id_type=MESH)
        for k in range(1, nx)]
    for c in xs:
        c.start()

    loads[5].wait()

    @pl.loop(0, na)
    def _(a):
        row = mean[a]
        high = row.astype(BF16).astype(F32)
        rest = row - high
        middle = rest.astype(BF16).astype(F32)
        fill = jnp.zeros((width - 3 * nbk, row.shape[1]), F32)
        stack = jnp.concatenate([high, middle, rest - middle, fill], axis=0)
        mean_t[a] = jnp.transpose(stack).astype(BF16)

    mean_out = pltpu.make_async_copy(mean_t, mean_th, i_sem.at[6])
    mean_out.start()

    for c in xs:
        c.wait_recv()
    st_sum[...] = st_own[...] + jnp.sum(st_x[...], axis=0)
    ys = [pltpu.make_async_remote_copy(
        src_ref=st_sum, dst_ref=st_y.at[k - 1], send_sem=y_send.at[k - 1],
        recv_sem=y_recv.at[k - 1], device_id=at(0, k), device_id_type=MESH)
        for k in range(1, ny)]
    for c in ys:
        c.start()
    loads[3].wait()
    loads[4].wait()
    for c in ys:
        c.wait_recv()
    total = jnp.sum(st_sum[...] + jnp.sum(st_y[...], axis=0), axis=1, keepdims=True)
    inflation = (width - 1) * total[1:2] / total[0:1]
    for i in range(na // 2):
        for c in ty_copies(i):
            c.wait_recv()
    for c in corner_copies():
        c.start()

    def listed_sum(a, b):
        acc = None
        for j in range(listed):
            code = nb[a, b, j]
            down = lax.shift_right_logical(code * 13, 6)
            block = grams[a + down, b + (code - 5 * down)].astype(F32)
            term = lw[a, b, j] * block
            acc = term if acc is None else acc + term
        return acc

    def unpack(acc):
        c = acc[:half]
        diag = acc[half:half + 1]
        vec = acc[half + 1:half + 2] + acc[half + 2:half + 3]
        flipped = jnp.transpose(jnp.concatenate([c, c], axis=0))
        top = jnp.where(hrow <= hlane, c, flipped[:half])
        shifted = pltpu.roll(c, half, 1)
        column = hlane - half
        corner = jnp.where(hrow > column, shifted, jnp.where(hrow == column, diag, flipped[:half]))
        bottom = jnp.where(column < 0, flipped[half:], corner)
        return jnp.concatenate([top, bottom], axis=0), vec

    def total_of(m):
        return jnp.sum(jnp.sum(m, axis=0, keepdims=True), axis=1, keepdims=True)

    def transform(groups):
        pairs = [unpack(listed_sum(a, b)) for a, b in groups]
        vecs = [v for _, v in pairs]
        ms = [jnp.where(eye, m + inflation, m) for m, _ in pairs]
        inv = [lax.rsqrt(total_of(m * m)) for m in ms]
        mid = [total_of(jnp.where(eye, m, 0.0)) * (1.0 / width) for m in ms]
        y = [(c * i, jnp.where(eye, m - c, m) * i) for m, i, c in zip(ms, inv, mid)]
        z2 = two_sweeps(y)
        v2 = [square(z) for z in z2]
        t2 = [scaled_by(product(p, v), 1.0 / 256) for p, v in zip(y, v2)]
        w = two_sweeps(t2)
        z4 = [product(z, u) for z, u in zip(z2, w)]
        v4 = [square(u) for u in w]
        t4 = [product(t, v) for t, v in zip(t2, v4)]
        z5 = [(z[0] * (768.0 - t[0]), (768.0 - t[0]) * z[1] - z[0] * t[1] - matmul(z[1], t[1]))
              for z, t in zip(z4, t4)]
        back = 1.0 / (256 * 512)
        z5 = [scaled_by(z, back) for z in z5]
        rb = [z[1].astype(BF16) for z in z5]
        x = [jnp.broadcast_to(v, (16, width)) for v in vecs]
        for _ in range(2):
            x = [z[0] * u + jnp.dot(u.astype(BF16), r, preferred_element_type=F32)
                 for z, u, r in zip(z5, x, rb)]
        shifts = [jnp.transpose(jnp.broadcast_to(u[0:1] * i, (width, width)))
                  for u, i in zip(x, inv)]
        for (a, b), (z, r), shift, i in zip(groups, z5, shifts, inv):
            scale = math.sqrt(width - 1) * jnp.sqrt(i)
            weight = scale * jnp.where(eye, r + z, r) + shift
            wts[a, b] = weight
            if b in (0, nbk - 1):
                wsend[a, b] = weight.astype(BF16)

    def w_copy(k, src, dst, dx, dy):
        return pltpu.make_async_remote_copy(
            src_ref=src, dst_ref=dst, send_sem=w_send.at[k], recv_sem=w_recv.at[k],
            device_id=at(dx, dy), device_id_type=MESH)

    def wx_copies():
        return [w_copy(0, wsend.at[na - 1], htx.at[0], 1, 0),
                w_copy(1, wsend.at[0], htx.at[1], -1, 0)]

    def wy_copies(k, first, count):
        rows = pl.ds(first, count)
        return [w_copy(k, wsend.at[rows, nbk - 1], hty.at[0, rows], 0, 1),
                w_copy(k + 1, wsend.at[rows, 0], hty.at[1, rows], 0, -1)]

    inner_wy = wy_copies(2, 2, na - 4)
    edge_wy = wy_copies(4, 0, 1) + wy_copies(6, na - 1, 1)
    last_wy = wy_copies(8, 1, 1) + wy_copies(10, na - 2, 1)
    inner = (na - 4) // 2

    @pl.loop(0, inner + 2)
    def _(i):
        h = i // inner
        r = i - inner * h

        @pl.when(i == inner)
        def _():
            for c in inner_wy:
                c.start()
            for c in tx_copies(own_cols, 0) + corner_copies():
                c.wait_recv()
            for k in range(HALO):
                for b in range(nbk + 2 * HALO):
                    grams[k, b] = landed[0, k, b]
                    grams[na + HALO + k, b] = landed[1, k, b]

        one = (1 - h) * (2 + 2 * r) + h * r
        two = (1 - h) * (3 + 2 * r) + h * (na - 1 - r)
        transform([(a, b) for a in (one, two) for b in range(nbk)])
        for b in range(1, nbk - 1):
            for a in (one, two):
                wsend[a, b] = wts[a, b].astype(BF16)

        @pl.when(i == inner)
        def _():
            for c in wx_copies() + edge_wy:
                c.start()

    for c in last_wy:
        c.start()

    def blend(a, b, lower, upper):
        left = wts[a, b - 1] if b > 0 else hty[0, a].astype(F32)
        right = wts[a, b + 1] if b < nbk - 1 else hty[1, a].astype(F32)
        out[a, b] = ((4.0 * wts[a, b] + (upper + lower) + (left + right)) * 0.125).astype(BF16)

    @pl.loop(1, na - 1)
    def _(a):
        for b in range(1, nbk - 1):
            blend(a, b, wts[a - 1, b], wts[a + 1, b])

    def row_out(a):
        return pltpu.make_async_copy(out.at[a], out_h.at[a], o_sem.at[a])

    for c in inner_wy + last_wy:
        c.wait_recv()

    @pl.loop(1, na - 1)
    def _(a):
        for b in (0, nbk - 1):
            blend(a, b, wts[a - 1, b], wts[a + 1, b])
        row_out(a).start()

    for c in edge_wy + wx_copies():
        c.wait_recv()
    for b in range(nbk):
        blend(0, b, htx[0, b].astype(F32), wts[1, b])
        blend(na - 1, b, wts[na - 2, b], htx[1, b].astype(F32))
    row_out(0).start()
    row_out(na - 1).start()
    for i in range(na // 2):
        for c in ty_copies(i):
            c.wait_send()
    for c in tx_copies(own_cols, 0) + corner_copies() + xs + ys + wx_copies() + inner_wy + edge_wy + last_wy:
        c.wait_send()
    mean_out.wait()
    for a in range(na):
        row_out(a).wait()


def apply_weights(members_h, mean_th, blended_h, out_h, members, mean_t, blended, result, sem):
    na, nbk, levels, width = members.shape
    row = lax.broadcasted_iota(jnp.int32, (width, width), 0)

    def loads(a):
        return [pltpu.make_async_copy(src.at[a], dst.at[a], sem.at[k, a])
                for k, (src, dst) in enumerate(
                    [(blended_h, blended), (mean_th, mean_t), (members_h, members)])]

    def copy_out(a):
        return pltpu.make_async_copy(result.at[a], out_h.at[a], sem.at[3, a])

    for a in range(na):
        for c in loads(a):
            c.start()

    @pl.loop(0, na)
    def _(a):
        for c in loads(a):
            c.wait()
        for b in range(nbk):
            pick = jnp.where((row == b) | (row == b + nbk) | (row == b + 2 * nbk), 1.0, 0.0)
            left = jnp.concatenate([members[a, b], mean_t[a]], axis=1)
            right = jnp.concatenate([blended[a, b], pick.astype(BF16)], axis=0)
            result[a, b] = jnp.dot(left, right, preferred_element_type=F32).astype(BF16)
        copy_out(a).start()

    @pl.loop(0, na)
    def _(a):
        copy_out(a).wait()


def shards(nx, ny, members, mean_state, obs_pert, obs_rinv, innovation, obs_count, neighbours,
           loc_weight):
    na, nbk, slots, width = obs_pert.shape
    levels = members.shape[2]
    hbm = pl.BlockSpec(memory_space=pltpu.HBM)
    dma = pltpu.SemaphoreType.DMA
    half = width // 2
    blended, mean_t = pl.pallas_call(
        functools.partial(analysis_weights, nx, ny),
        out_shape=[
            jax.ShapeDtypeStruct((na, nbk, width, width), BF16),
            jax.ShapeDtypeStruct((na, levels, width), BF16),
        ],
        in_specs=[hbm] * 7,
        out_specs=[hbm] * 2,
        scratch_shapes=[
            pltpu.VMEM((na, nbk, width, width), BF16),
            pltpu.VMEM((na, levels, width), BF16),
            pltpu.SMEM((nbk, na), jnp.int32),
            pltpu.SMEM(neighbours.shape, jnp.int32),
            pltpu.SMEM(loc_weight.shape, F32),
            pltpu.VMEM(obs_pert.shape, BF16),
            pltpu.VMEM(obs_rinv.shape, BF16),
            pltpu.VMEM(innovation.shape, BF16),
            pltpu.VMEM(mean_state.shape, F32),
            pltpu.VMEM((na + 2 * HALO, nbk + 2 * HALO, half + 16, width), BF16),
            pltpu.VMEM((2, HALO, nbk + 2 * HALO, half + 16, width), BF16),
            pltpu.VMEM((na, nbk, width, width), F32),
            pltpu.VMEM((na, nbk, width, width), BF16),
            pltpu.VMEM((2, nbk, width, width), BF16),
            pltpu.VMEM((2, na, width, width), BF16),
            pltpu.VMEM((8, slots), F32),
            pltpu.VMEM((nx - 1, 8, slots), F32),
            pltpu.VMEM((8, slots), F32),
            pltpu.VMEM((ny - 1, 8, slots), F32),
            dma((7,)), dma((na // 2,)), dma((na,)),
            dma((6 + na,)), dma((6 + na,)),
            dma((nx - 1,)), dma((nx - 1,)),
            dma((ny - 1,)), dma((ny - 1,)),
            dma((12,)), dma((12,)),
        ],
        compiler_params=pltpu.CompilerParams(
            collective_id=0, has_side_effects=True, vmem_limit_bytes=57 * 1024 * 1024),
    )(obs_count.T, neighbours, loc_weight, obs_pert, obs_rinv, innovation, mean_state)
    return pl.pallas_call(
        apply_weights,
        out_shape=jax.ShapeDtypeStruct(members.shape, BF16),
        in_specs=[hbm] * 3,
        out_specs=hbm,
        scratch_shapes=[
            pltpu.VMEM(members.shape, BF16),
            pltpu.VMEM((na, levels, width), BF16),
            pltpu.VMEM((na, nbk, width, width), BF16),
            pltpu.VMEM(members.shape, BF16),
            dma((4, na)),
        ],
        compiler_params=pltpu.CompilerParams(vmem_limit_bytes=57 * 1024 * 1024),
    )(members, mean_t, blended)


def solution(mesh):
    nx, ny = mesh.shape["tx"], mesh.shape["ty"]
    return jax.shard_map(
        functools.partial(shards, nx, ny),
        mesh=mesh,
        in_specs=(
            P("tx", "ty", None, None),
            P("tx", "ty", None),
            P("tx", "ty", None, None),
            P("tx", "ty", None),
            P("tx", "ty", None),
            P("tx", "ty"),
            P("tx", "ty", None),
            P("tx", "ty", None),
        ),
        out_specs=P("tx", "ty", None, None),
        check_vma=False,
    )
```

```python
import functools
import math

import jax
import jax.numpy as jnp
from jax import lax
from jax.experimental import pallas as pl
from jax.experimental.pallas import tpu as pltpu
from jax.sharding import PartitionSpec as P

MESH = pl.DeviceIdType.MESH
HALO = 2
F32 = jnp.float32
BF16 = jnp.bfloat16


def offsets(nx, ny):
    found = {(dx, 0) for dx in range(1, nx)} | {(0, dy) for dy in range(1, ny)}
    found |= {(dx % nx, dy % ny) for dx in (-1, 1) for dy in (-1, 1)}
    return sorted(found - {(0, 0)})


def matmul(a, b):
    return jnp.dot(a.astype(BF16), b.astype(BF16), preferred_element_type=F32)


def square(x):
    s, a = x
    return s * s, matmul(a, a) + (2.0 * s) * a


def product(left, right):
    s, a = left
    t, b = right
    return s * t, matmul(a, b) + (s * b + t * a)


def two_sweeps(y, beside):
    sq = [square(v) for v in y]
    beside()
    inner = [q[1] - 9.0 * v[1] for q, v in zip(sq, y)]
    cross = [matmul(q[1], i) for q, i in zip(sq, inner)]
    beside()
    out = []
    for c, q, v in zip(cross, sq, y):
        mid = q[0] - 9.0 * v[0] + 27.0
        out.append((q[0] * mid - 39.0 * v[0] + 36.0,
                    c + ((mid + q[0]) * q[1] - (9.0 * q[0] + 39.0) * v[1])))
    return out


def scaled_by(x, factor):
    return x[0] * factor, x[1] * factor


def analysis_weights(nx, ny, cnt_h, nb_h, lw_h, pert_h, rinv_h, innov_h, mean_h,
                     out_h, mean_th,
                     out, mean_t, cnt, nb, lw, pert, rinv, innov, mean,
                     grams, landed, ready, ready_v, wts, wsend, htx, hty, st_own, st_x, st_sum, st_y,
                     i_sem, p_sem, o_sem, g_send, g_recv, x_send, x_recv, y_send, y_recv,
                     w_send, w_recv):
    na, nbk, slots, width = pert.shape
    listed = nb.shape[2]
    half = width // 2
    mx, my = lax.axis_index("tx"), lax.axis_index("ty")

    def at(dx, dy):
        return {"tx": lax.rem(mx + (dx % nx), nx), "ty": lax.rem(my + (dy % ny), ny)}

    barrier = pltpu.get_barrier_semaphore()
    partners = offsets(nx, ny)
    for dx, dy in partners:
        pl.semaphore_signal(barrier, inc=1, device_id=at(dx, dy), device_id_type=MESH)

    def pair_at(i):
        h = i // 2
        return (1 - h) * (na - 2) * i + h * 2 * (i - 1)

    loads = [pltpu.make_async_copy(src, dst, i_sem.at[k]) for k, (src, dst) in enumerate([
        (cnt_h, cnt), (rinv_h, rinv), (innov_h, innov), (nb_h, nb), (lw_h, lw), (mean_h, mean)])]
    for c in loads[:3]:
        c.start()

    def pert_load(i):
        rows = pl.ds(pair_at(i), 2)
        return pltpu.make_async_copy(pert_h.at[rows], pert.at[rows], p_sem.at[i])

    for i in range(na // 2):
        pert_load(i).start()
    for c in loads[3:]:
        c.start()
    for c in loads[:3]:
        c.wait()

    lane = lax.broadcasted_iota(jnp.int32, (1, slots), 1)
    eye = (lax.broadcasted_iota(jnp.int32, (width, width), 0)
           == lax.broadcasted_iota(jnp.int32, (width, width), 1))
    hrow = lax.broadcasted_iota(jnp.int32, (half, width), 0)
    hlane = lax.broadcasted_iota(jnp.int32, (half, width), 1)
    sub = lax.broadcasted_iota(jnp.int32, (16, slots), 0)
    subw = lax.broadcasted_iota(jnp.int32, (16, width), 0)

    def gram_terms(blocks):
        ps = [pert[a, b] for a, b in blocks]
        lives = [lane < cnt[b, a] for a, b in blocks]
        qs = [jnp.where(live, rinv[a, b:b + 1, :].astype(F32), 0.0)
              for live, (a, b) in zip(lives, blocks)]
        ds = [innov[a, b:b + 1, :].astype(F32) for a, b in blocks]
        flipped = [jnp.transpose(p) for p in ps]
        scaled = [(f.astype(F32) * q).astype(BF16) for f, q in zip(flipped, qs)]
        qds = [q * d for q, d in zip(qs, ds)]
        his = [qd.astype(BF16).astype(F32) for qd in qds]
        tails = [jnp.where(sub == 0, hi, jnp.where(sub == 1, qd - hi, 0.0)).astype(BF16)
                 for hi, qd in zip(his, qds)]
        gs = [jnp.dot(x, p, preferred_element_type=F32) for x, p in zip(scaled, ps)]
        vs = [jnp.dot(x, p, preferred_element_type=F32) for x, p in zip(tails, ps)]
        diags = [jnp.sum(jnp.where(eye, g, 0.0), axis=0, keepdims=True) for g in gs]
        lowers = [pltpu.roll(g[half:], half, 1) for g in gs]
        packed = [jnp.where(hrow <= hlane, g[:half], lower) for g, lower in zip(gs, lowers)]
        first = second = 0.0
        for (a, b), pk, v, diag, qd, d, live in zip(blocks, packed, vs, diags, qds, ds, lives):
            vec = v[0:1] + v[1:2]
            vhi = vec.astype(BF16).astype(F32)
            extra = jnp.where(subw == 0, diag,
                              jnp.where(subw == 1, vhi, jnp.where(subw == 2, vec - vhi, 0.0)))
            grams[a + HALO, b + HALO, :half, :] = pk.astype(BF16)
            grams[a + HALO, b + HALO, half:, :] = extra.astype(BF16)
            first = first + qd * d
            second = second + (jnp.where(live, 1.0, 0.0) + diag * (1.0 / (width - 1)))
        return first, second

    def remote(src, dst, k, dx, dy):
        return pltpu.make_async_remote_copy(
            src_ref=src, dst_ref=dst, send_sem=g_send.at[k], recv_sem=g_recv.at[k],
            device_id=at(dx, dy), device_id_type=MESH)

    own_cols = pl.ds(HALO, nbk)
    ends = (pl.ds(0, HALO), pl.ds(nbk + HALO, HALO))

    def tx_copies(src_cols, dst_cols, k, dy):
        return [
            remote(grams.at[pl.ds(na, HALO), src_cols], landed.at[0, :, dst_cols], k, 1, dy),
            remote(grams.at[pl.ds(HALO, HALO), src_cols], landed.at[1, :, dst_cols], k + 1, -1, dy)]

    def ty_copies(i):
        rows = pl.ds(HALO + pair_at(i), 2)
        k = 6 + 2 * i
        return [remote(grams.at[rows, pl.ds(nbk, HALO)], grams.at[rows, ends[0]], k, 0, 1),
                remote(grams.at[rows, pl.ds(HALO, HALO)], grams.at[rows, ends[1]], k + 1, 0, -1)]

    def corner_copies():
        return (tx_copies(pl.ds(nbk, HALO), ends[0], 2, 1)
                + tx_copies(pl.ds(HALO, HALO), ends[1], 4, -1))

    def gram_rows(i, sums):
        first, second = sums
        pert_load(i).wait()
        base = pair_at(i)
        one, two = gram_terms([(base + k, b) for k in range(2) for b in range(nbk)])

        @pl.when(i == 1)
        def _():
            pl.semaphore_wait(barrier, len(partners))
            for c in ty_copies(0) + tx_copies(own_cols, own_cols, 0, 0):
                c.start()

        @pl.when(i >= 1)
        def _():
            for c in ty_copies(i):
                c.start()

        return first + one, second + two

    zero = jnp.zeros((1, slots), F32)
    sums = lax.fori_loop(0, na // 2, gram_rows, (zero, zero))
    rows8 = lax.broadcasted_iota(jnp.int32, (8, slots), 0)
    st_own[...] = jnp.where(rows8 == 0, sums[0], jnp.where(rows8 == 1, sums[1], 0.0))
    xs = [pltpu.make_async_remote_copy(
        src_ref=st_own, dst_ref=st_x.at[k - 1], send_sem=x_send.at[k - 1],
        recv_sem=x_recv.at[k - 1], device_id=at(k, 0), device_id_type=MESH)
        for k in range(1, nx)]
    for c in xs + corner_copies():
        c.start()

    loads[5].wait()

    @pl.loop(0, na)
    def _(a):
        row = mean[a]
        high = row.astype(BF16).astype(F32)
        rest = row - high
        middle = rest.astype(BF16).astype(F32)
        fill = jnp.zeros((width - 3 * nbk, row.shape[1]), F32)
        stack = jnp.concatenate([high, middle, rest - middle, fill], axis=0)
        mean_t[a] = jnp.transpose(stack).astype(BF16)

    mean_out = pltpu.make_async_copy(mean_t, mean_th, i_sem.at[6])
    mean_out.start()

    for c in xs:
        c.wait_recv()
    st_sum[...] = st_own[...] + jnp.sum(st_x[...], axis=0)
    ys = [pltpu.make_async_remote_copy(
        src_ref=st_sum, dst_ref=st_y.at[k - 1], send_sem=y_send.at[k - 1],
        recv_sem=y_recv.at[k - 1], device_id=at(0, k), device_id_type=MESH)
        for k in range(1, ny)]
    for c in ys:
        c.start()
    loads[3].wait()
    loads[4].wait()
    for i in range(na // 2):
        for c in ty_copies(i):
            c.wait_recv()

    def listed_sum(a, b):
        acc = None
        for j in range(listed):
            code = nb[a, b, j]
            down = lax.shift_right_logical(code * 13, 6)
            block = grams[a + down, b + (code - 5 * down)].astype(F32)
            term = lw[a, b, j] * block
            acc = term if acc is None else acc + term
        return acc

    def unpack(acc):
        c = acc[:half]
        diag = acc[half:half + 1]
        vec = acc[half + 1:half + 2] + acc[half + 2:half + 3]
        flipped = jnp.transpose(jnp.concatenate([c, c], axis=0))
        top = jnp.where(hrow <= hlane, c, flipped[:half])
        shifted = pltpu.roll(c, half, 1)
        column = hlane - half
        corner = jnp.where(hrow > column, shifted, jnp.where(hrow == column, diag, flipped[:half]))
        bottom = jnp.where(column < 0, flipped[half:], corner)
        return jnp.concatenate([top, bottom], axis=0), vec

    def total_of(m):
        return jnp.sum(jnp.sum(m, axis=0, keepdims=True), axis=1, keepdims=True)

    def prepare(k, slot, group):
        m, vec = unpack(listed_sum(*group))
        ready[slot, k] = m
        ready_v[slot, k] = jnp.broadcast_to(vec, (8, width))

    def transform(groups, slot, later):
        todo = list(enumerate(later))

        def beside():
            if todo:
                prepare(todo[0][0], 1 - slot, todo.pop(0)[1])

        ms = [ready[slot, k] for k in range(len(groups))]
        vecs = [ready_v[slot, k][0:1] for k in range(len(groups))]
        ms = [jnp.where(eye, m + inflation, m) for m in ms]
        inv = [lax.rsqrt(total_of(m * m)) for m in ms]
        mid = [total_of(jnp.where(eye, m, 0.0)) * (1.0 / width) for m in ms]
        y = [(c * i, jnp.where(eye, m - c, m) * i) for m, i, c in zip(ms, inv, mid)]
        z2 = two_sweeps(y, beside)
        v2 = [square(z) for z in z2]
        beside()
        t2 = [scaled_by(product(p, v), 1.0 / 256) for p, v in zip(y, v2)]
        beside()
        w = two_sweeps(t2, beside)
        z4 = [product(z, u) for z, u in zip(z2, w)]
        v4 = [square(u) for u in w]
        beside()
        t4 = [product(t, v) for t, v in zip(t2, v4)]
        beside()
        z5 = [(z[0] * (768.0 - t[0]), (768.0 - t[0]) * z[1] - z[0] * t[1] - matmul(z[1], t[1]))
              for z, t in zip(z4, t4)]
        while todo:
            beside()
        back = 1.0 / (256 * 512)
        z5 = [scaled_by(z, back) for z in z5]
        rb = [z[1].astype(BF16) for z in z5]
        x = [jnp.broadcast_to(v, (16, width)) for v in vecs]
        for _ in range(2):
            x = [z[0] * u + jnp.dot(u.astype(BF16), r, preferred_element_type=F32)
                 for z, u, r in zip(z5, x, rb)]
        shifts = [jnp.transpose(jnp.broadcast_to(u[0:1] * i, (width, width)))
                  for u, i in zip(x, inv)]
        for (a, b), (z, r), shift, i in zip(groups, z5, shifts, inv):
            scale = math.sqrt(width - 1) * jnp.sqrt(i)
            weight = scale * jnp.where(eye, r + z, r) + shift
            wts[a, b] = weight
            wsend[a, b] = weight.astype(BF16)

    def w_copy(k, src, dst, dx, dy):
        return pltpu.make_async_remote_copy(
            src_ref=src, dst_ref=dst, send_sem=w_send.at[k], recv_sem=w_recv.at[k],
            device_id=at(dx, dy), device_id_type=MESH)

    def wx_copies():
        return [w_copy(0, wsend.at[na - 1], htx.at[0], 1, 0),
                w_copy(1, wsend.at[0], htx.at[1], -1, 0)]

    def wy_copies(k, first, count):
        rows = pl.ds(first, count)
        return [w_copy(k, wsend.at[rows, nbk - 1], hty.at[0, rows], 0, 1),
                w_copy(k + 1, wsend.at[rows, 0], hty.at[1, rows], 0, -1)]

    inner_wy = wy_copies(2, 2, na - 4)
    edge_wy = wy_copies(4, 0, 1) + wy_copies(6, na - 1, 1)
    last_wy = wy_copies(8, 1, 1) + wy_copies(10, na - 2, 1)
    inner = (na - 4) // 2

    def batch(i):
        h = i // inner
        r = i - inner * h
        one = (1 - h) * (2 + 2 * r) + h * r
        two = (1 - h) * (3 + 2 * r) + h * (na - 1 - r)
        return [(a, b) for a in (one, two) for b in range(nbk)]

    for k, group in enumerate(batch(0)):
        prepare(k, 0, group)
    for c in ys:
        c.wait_recv()
    total = jnp.sum(st_sum[...] + jnp.sum(st_y[...], axis=0), axis=1, keepdims=True)
    inflation = (width - 1) * total[1:2] / total[0:1]

    @pl.loop(0, inner + 2)
    def _(i):
        @pl.when(i == inner - 1)
        def _():
            for c in tx_copies(own_cols, own_cols, 0, 0) + corner_copies():
                c.wait_recv()
            for k in range(HALO):
                for b in range(nbk + 2 * HALO):
                    grams[k, b] = landed[0, k, b]
                    grams[na + HALO + k, b] = landed[1, k, b]

        @pl.when(i == inner)
        def _():
            for c in inner_wy:
                c.start()

        transform(batch(i), i % 2, batch(i + 1 - (i + 1) // (inner + 2)))

        @pl.when(i == inner)
        def _():
            for c in wx_copies() + edge_wy:
                c.start()

    for c in last_wy:
        c.start()

    def blend(a, b, lower, upper):
        left = wts[a, b - 1] if b > 0 else hty[0, a].astype(F32)
        right = wts[a, b + 1] if b < nbk - 1 else hty[1, a].astype(F32)
        out[a, b] = ((4.0 * wts[a, b] + (upper + lower) + (left + right)) * 0.125).astype(BF16)

    @pl.loop(1, na - 1)
    def _(a):
        for b in range(1, nbk - 1):
            blend(a, b, wts[a - 1, b], wts[a + 1, b])

    def row_out(a):
        return pltpu.make_async_copy(out.at[a], out_h.at[a], o_sem.at[a])

    for c in inner_wy + last_wy:
        c.wait_recv()

    @pl.loop(1, na - 1)
    def _(a):
        for b in (0, nbk - 1):
            blend(a, b, wts[a - 1, b], wts[a + 1, b])
        row_out(a).start()

    for c in edge_wy + wx_copies():
        c.wait_recv()
    for b in range(nbk):
        blend(0, b, htx[0, b].astype(F32), wts[1, b])
        blend(na - 1, b, wts[na - 2, b], htx[1, b].astype(F32))
    row_out(0).start()
    row_out(na - 1).start()
    for i in range(na // 2):
        for c in ty_copies(i):
            c.wait_send()
    for c in tx_copies(own_cols, own_cols, 0, 0) + corner_copies() + xs + ys + wx_copies() + inner_wy + edge_wy + last_wy:
        c.wait_send()
    mean_out.wait()
    for a in range(na):
        row_out(a).wait()


def apply_weights(members_h, mean_th, blended_h, out_h, members, mean_t, blended, result, sem):
    na, nbk, levels, width = members.shape
    row = lax.broadcasted_iota(jnp.int32, (width, width), 0)

    def loads(a):
        return [pltpu.make_async_copy(src.at[a], dst.at[a], sem.at[k, a])
                for k, (src, dst) in enumerate(
                    [(blended_h, blended), (mean_th, mean_t), (members_h, members)])]

    def copy_out(a):
        return pltpu.make_async_copy(result.at[a], out_h.at[a], sem.at[3, a])

    for a in range(na):
        for c in loads(a):
            c.start()

    @pl.loop(0, na)
    def _(a):
        for c in loads(a):
            c.wait()
        for b in range(nbk):
            pick = jnp.where((row == b) | (row == b + nbk) | (row == b + 2 * nbk), 1.0, 0.0)
            left = jnp.concatenate([members[a, b], mean_t[a]], axis=1)
            right = jnp.concatenate([blended[a, b], pick.astype(BF16)], axis=0)
            result[a, b] = jnp.dot(left, right, preferred_element_type=F32).astype(BF16)
        copy_out(a).start()

    @pl.loop(0, na)
    def _(a):
        copy_out(a).wait()


def shards(nx, ny, members, mean_state, obs_pert, obs_rinv, innovation, obs_count, neighbours,
           loc_weight):
    na, nbk, slots, width = obs_pert.shape
    levels = members.shape[2]
    hbm = pl.BlockSpec(memory_space=pltpu.HBM)
    dma = pltpu.SemaphoreType.DMA
    half = width // 2
    blended, mean_t = pl.pallas_call(
        functools.partial(analysis_weights, nx, ny),
        out_shape=[
            jax.ShapeDtypeStruct((na, nbk, width, width), BF16),
            jax.ShapeDtypeStruct((na, levels, width), BF16),
        ],
        in_specs=[hbm] * 7,
        out_specs=[hbm] * 2,
        scratch_shapes=[
            pltpu.VMEM((na, nbk, width, width), BF16),
            pltpu.VMEM((na, levels, width), BF16),
            pltpu.SMEM((nbk, na), jnp.int32),
            pltpu.SMEM(neighbours.shape, jnp.int32),
            pltpu.SMEM(loc_weight.shape, F32),
            pltpu.VMEM(obs_pert.shape, BF16),
            pltpu.VMEM(obs_rinv.shape, BF16),
            pltpu.VMEM(innovation.shape, BF16),
            pltpu.VMEM(mean_state.shape, F32),
            pltpu.VMEM((na + 2 * HALO, nbk + 2 * HALO, half + 16, width), BF16),
            pltpu.VMEM((2, HALO, nbk + 2 * HALO, half + 16, width), BF16),
            pltpu.VMEM((2, 2 * nbk, width, width), F32),
            pltpu.VMEM((2, 2 * nbk, 8, width), F32),
            pltpu.VMEM((na, nbk, width, width), F32),
            pltpu.VMEM((na, nbk, width, width), BF16),
            pltpu.VMEM((2, nbk, width, width), BF16),
            pltpu.VMEM((2, na, width, width), BF16),
            pltpu.VMEM((8, slots), F32),
            pltpu.VMEM((nx - 1, 8, slots), F32),
            pltpu.VMEM((8, slots), F32),
            pltpu.VMEM((ny - 1, 8, slots), F32),
            dma((7,)), dma((na // 2,)), dma((na,)),
            dma((6 + na,)), dma((6 + na,)),
            dma((nx - 1,)), dma((nx - 1,)),
            dma((ny - 1,)), dma((ny - 1,)),
            dma((12,)), dma((12,)),
        ],
        compiler_params=pltpu.CompilerParams(
            collective_id=0, has_side_effects=True, vmem_limit_bytes=57 * 1024 * 1024),
    )(obs_count.T, neighbours, loc_weight, obs_pert, obs_rinv, innovation, mean_state)
    return pl.pallas_call(
        apply_weights,
        out_shape=jax.ShapeDtypeStruct(members.shape, BF16),
        in_specs=[hbm] * 3,
        out_specs=hbm,
        scratch_shapes=[
            pltpu.VMEM(members.shape, BF16),
            pltpu.VMEM((na, levels, width), BF16),
            pltpu.VMEM((na, nbk, width, width), BF16),
            pltpu.VMEM(members.shape, BF16),
            dma((4, na)),
        ],
        compiler_params=pltpu.CompilerParams(vmem_limit_bytes=57 * 1024 * 1024),
    )(members, mean_t, blended)


def solution(mesh):
    nx, ny = mesh.shape["tx"], mesh.shape["ty"]
    return jax.shard_map(
        functools.partial(shards, nx, ny),
        mesh=mesh,
        in_specs=(
            P("tx", "ty", None, None),
            P("tx", "ty", None),
            P("tx", "ty", None, None),
            P("tx", "ty", None),
            P("tx", "ty", None),
            P("tx", "ty"),
            P("tx", "ty", None),
            P("tx", "ty", None),
        ),
        out_specs=P("tx", "ty", None, None),
        check_vma=False,
    )
```

```python
import functools
import math

import jax
import jax.numpy as jnp
from jax import lax
from jax.experimental import pallas as pl
from jax.experimental.pallas import tpu as pltpu
from jax.sharding import PartitionSpec as P

MESH = pl.DeviceIdType.MESH
HALO = 2
F32 = jnp.float32
BF16 = jnp.bfloat16


def offsets(nx, ny):
    return [(dx, 0) for dx in range(1, nx)] + [(0, dy) for dy in range(1, ny)]


def matmul(a, b):
    return jnp.dot(a.astype(BF16), b.astype(BF16), preferred_element_type=F32)


def square(x):
    s, a = x
    return s * s, matmul(a, a) + (2.0 * s) * a


def product(left, right):
    s, a = left
    t, b = right
    return s * t, matmul(a, b) + (s * b + t * a)


def two_sweeps(y, beside):
    sq = [square(v) for v in y]
    beside()
    inner = [q[1] - 9.0 * v[1] for q, v in zip(sq, y)]
    cross = [matmul(q[1], i) for q, i in zip(sq, inner)]
    beside()
    out = []
    for c, q, v in zip(cross, sq, y):
        mid = q[0] - 9.0 * v[0] + 27.0
        out.append((q[0] * mid - 39.0 * v[0] + 36.0,
                    c + ((mid + q[0]) * q[1] - (9.0 * q[0] + 39.0) * v[1])))
    return out


def scaled_by(x, factor):
    return x[0] * factor, x[1] * factor


def analysis_weights(nx, ny, cnt_h, nb_h, lw_h, pert_h, rinv_h, innov_h, mean_h,
                     out_h, mean_th,
                     out, mean_t, cnt, nb, lw, pert, rinv, innov, mean,
                     grams, landed, ready, ready_v, wts, wsend, htx, hty, st_own, st_x, st_sum, st_y,
                     i_sem, p_sem, o_sem, g_send, g_recv, x_send, x_recv, y_send, y_recv,
                     w_send, w_recv):
    na, nbk, slots, width = pert.shape
    listed = nb.shape[2]
    half = width // 2
    mx, my = lax.axis_index("tx"), lax.axis_index("ty")

    def at(dx, dy):
        return {"tx": lax.rem(mx + (dx % nx), nx), "ty": lax.rem(my + (dy % ny), ny)}

    barrier = pltpu.get_barrier_semaphore()
    partners = offsets(nx, ny)
    for dx, dy in partners:
        pl.semaphore_signal(barrier, inc=1, device_id=at(dx, dy), device_id_type=MESH)

    def pair_at(i):
        h = i // 2
        return (1 - h) * (na - 2) * i + h * 2 * (i - 1)

    loads = [pltpu.make_async_copy(src, dst, i_sem.at[k]) for k, (src, dst) in enumerate([
        (cnt_h, cnt), (rinv_h, rinv), (innov_h, innov), (nb_h, nb), (lw_h, lw), (mean_h, mean)])]
    for c in loads[:3]:
        c.start()

    def pert_load(i):
        rows = pl.ds(pair_at(i), 2)
        return pltpu.make_async_copy(pert_h.at[rows], pert.at[rows], p_sem.at[i])

    for i in range(na // 2):
        pert_load(i).start()
    for c in loads[3:]:
        c.start()
    for c in loads[:3]:
        c.wait()

    lane = lax.broadcasted_iota(jnp.int32, (1, slots), 1)
    eye = (lax.broadcasted_iota(jnp.int32, (width, width), 0)
           == lax.broadcasted_iota(jnp.int32, (width, width), 1))
    hrow = lax.broadcasted_iota(jnp.int32, (half, width), 0)
    hlane = lax.broadcasted_iota(jnp.int32, (half, width), 1)
    sub = lax.broadcasted_iota(jnp.int32, (16, slots), 0)
    subw = lax.broadcasted_iota(jnp.int32, (16, width), 0)

    def gram_terms(blocks):
        ps = [pert[a, b] for a, b in blocks]
        lives = [lane < cnt[b, a] for a, b in blocks]
        qs = [jnp.where(live, rinv[a, b:b + 1, :].astype(F32), 0.0)
              for live, (a, b) in zip(lives, blocks)]
        ds = [innov[a, b:b + 1, :].astype(F32) for a, b in blocks]
        flipped = [jnp.transpose(p) for p in ps]
        scaled = [(f.astype(F32) * q).astype(BF16) for f, q in zip(flipped, qs)]
        qds = [q * d for q, d in zip(qs, ds)]
        his = [qd.astype(BF16).astype(F32) for qd in qds]
        tails = [jnp.where(sub == 0, hi, jnp.where(sub == 1, qd - hi, 0.0)).astype(BF16)
                 for hi, qd in zip(his, qds)]
        gs = [jnp.dot(x, p, preferred_element_type=F32) for x, p in zip(scaled, ps)]
        vs = [jnp.dot(x, p, preferred_element_type=F32) for x, p in zip(tails, ps)]
        diags = [jnp.sum(jnp.where(eye, g, 0.0), axis=0, keepdims=True) for g in gs]
        lowers = [pltpu.roll(g[half:], half, 1) for g in gs]
        packed = [jnp.where(hrow <= hlane, g[:half], lower) for g, lower in zip(gs, lowers)]
        first = second = 0.0
        for (a, b), pk, v, diag, qd, d, live in zip(blocks, packed, vs, diags, qds, ds, lives):
            vec = v[0:1] + v[1:2]
            vhi = vec.astype(BF16).astype(F32)
            extra = jnp.where(subw == 0, diag,
                              jnp.where(subw == 1, vhi, jnp.where(subw == 2, vec - vhi, 0.0)))
            grams[a + HALO, b + HALO, :half, :] = pk.astype(BF16)
            grams[a + HALO, b + HALO, half:, :] = extra.astype(BF16)
            first = first + qd * d
            second = second + (jnp.where(live, 1.0, 0.0) + diag * (1.0 / (width - 1)))
        return first, second

    def remote(src, dst, k, dx, dy):
        return pltpu.make_async_remote_copy(
            src_ref=src, dst_ref=dst, send_sem=g_send.at[k], recv_sem=g_recv.at[k],
            device_id=at(dx, dy), device_id_type=MESH)

    own_cols = pl.ds(HALO, nbk)
    ends = (pl.ds(0, HALO), pl.ds(nbk + HALO, HALO))

    def tx_copies():
        return [
            remote(grams.at[pl.ds(na, HALO), own_cols], landed.at[0, :, own_cols], 0, 1, 0),
            remote(grams.at[pl.ds(HALO, HALO), own_cols], landed.at[1, :, own_cols], 1, -1, 0)]

    def ty_copies(i):
        rows = pl.ds(HALO + pair_at(i), 2)
        k = 4 + 2 * i
        return [remote(grams.at[rows, pl.ds(nbk, HALO)], grams.at[rows, ends[0]], k, 0, 1),
                remote(grams.at[rows, pl.ds(HALO, HALO)], grams.at[rows, ends[1]], k + 1, 0, -1)]

    def corner_copies():
        return [remote(landed.at[:, :, pl.ds(nbk, HALO)], landed.at[:, :, ends[0]], 2, 0, 1),
                remote(landed.at[:, :, pl.ds(HALO, HALO)], landed.at[:, :, ends[1]], 3, 0, -1)]

    def gram_rows(i, sums):
        first, second = sums
        pert_load(i).wait()
        base = pair_at(i)
        one, two = gram_terms([(base + k, b) for k in range(2) for b in range(nbk)])

        @pl.when(i == 1)
        def _():
            pl.semaphore_wait(barrier, len(partners))
            for c in ty_copies(0) + tx_copies():
                c.start()

        @pl.when(i >= 1)
        def _():
            for c in ty_copies(i):
                c.start()

        return first + one, second + two

    zero = jnp.zeros((1, slots), F32)
    sums = lax.fori_loop(0, na // 2, gram_rows, (zero, zero))
    rows8 = lax.broadcasted_iota(jnp.int32, (8, slots), 0)
    st_own[...] = jnp.where(rows8 == 0, sums[0], jnp.where(rows8 == 1, sums[1], 0.0))
    xs = [pltpu.make_async_remote_copy(
        src_ref=st_own, dst_ref=st_x.at[k - 1], send_sem=x_send.at[k - 1],
        recv_sem=x_recv.at[k - 1], device_id=at(k, 0), device_id_type=MESH)
        for k in range(1, nx)]
    for c in xs:
        c.start()

    loads[5].wait()

    @pl.loop(0, na)
    def _(a):
        row = mean[a]
        high = row.astype(BF16).astype(F32)
        rest = row - high
        middle = rest.astype(BF16).astype(F32)
        fill = jnp.zeros((width - 3 * nbk, row.shape[1]), F32)
        stack = jnp.concatenate([high, middle, rest - middle, fill], axis=0)
        mean_t[a] = jnp.transpose(stack).astype(BF16)

    mean_out = pltpu.make_async_copy(mean_t, mean_th, i_sem.at[6])
    mean_out.start()

    for c in xs:
        c.wait_recv()
    st_sum[...] = st_own[...] + jnp.sum(st_x[...], axis=0)
    ys = [pltpu.make_async_remote_copy(
        src_ref=st_sum, dst_ref=st_y.at[k - 1], send_sem=y_send.at[k - 1],
        recv_sem=y_recv.at[k - 1], device_id=at(0, k), device_id_type=MESH)
        for k in range(1, ny)]
    for c in ys:
        c.start()
    loads[3].wait()
    loads[4].wait()
    for i in range(na // 2):
        for c in ty_copies(i):
            c.wait_recv()
    for c in tx_copies():
        c.wait_recv()
    for c in corner_copies():
        c.start()

    def listed_sum(a, b):
        acc = None
        for j in range(listed):
            code = nb[a, b, j]
            down = lax.shift_right_logical(code * 13, 6)
            block = grams[a + down, b + (code - 5 * down)].astype(F32)
            term = lw[a, b, j] * block
            acc = term if acc is None else acc + term
        return acc

    def unpack(acc):
        c = acc[:half]
        diag = acc[half:half + 1]
        vec = acc[half + 1:half + 2] + acc[half + 2:half + 3]
        flipped = jnp.transpose(jnp.concatenate([c, c], axis=0))
        top = jnp.where(hrow <= hlane, c, flipped[:half])
        shifted = pltpu.roll(c, half, 1)
        column = hlane - half
        corner = jnp.where(hrow > column, shifted, jnp.where(hrow == column, diag, flipped[:half]))
        bottom = jnp.where(column < 0, flipped[half:], corner)
        return jnp.concatenate([top, bottom], axis=0), vec

    def total_of(m):
        return jnp.sum(jnp.sum(m, axis=0, keepdims=True), axis=1, keepdims=True)

    def prepare(k, slot, group):
        m, vec = unpack(listed_sum(*group))
        ready[slot, k] = m
        ready_v[slot, k] = jnp.broadcast_to(vec, (8, width))

    def transform(groups, slot, later):
        todo = list(enumerate(later))

        def beside():
            if todo:
                prepare(todo[0][0], 1 - slot, todo.pop(0)[1])

        ms = [ready[slot, k] for k in range(len(groups))]
        vecs = [ready_v[slot, k][0:1] for k in range(len(groups))]
        ms = [jnp.where(eye, m + inflation, m) for m in ms]
        inv = [lax.rsqrt(total_of(m * m)) for m in ms]
        mid = [total_of(jnp.where(eye, m, 0.0)) * (1.0 / width) for m in ms]
        y = [(c * i, jnp.where(eye, m - c, m) * i) for m, i, c in zip(ms, inv, mid)]
        z2 = two_sweeps(y, beside)
        v2 = [square(z) for z in z2]
        beside()
        t2 = [scaled_by(product(p, v), 1.0 / 256) for p, v in zip(y, v2)]
        beside()
        w = two_sweeps(t2, beside)
        z4 = [product(z, u) for z, u in zip(z2, w)]
        v4 = [square(u) for u in w]
        beside()
        t4 = [product(t, v) for t, v in zip(t2, v4)]
        beside()
        z5 = [(z[0] * (768.0 - t[0]), (768.0 - t[0]) * z[1] - z[0] * t[1] - matmul(z[1], t[1]))
              for z, t in zip(z4, t4)]
        while todo:
            beside()
        back = 1.0 / (256 * 512)
        z5 = [scaled_by(z, back) for z in z5]
        rb = [z[1].astype(BF16) for z in z5]
        x = [jnp.broadcast_to(v, (16, width)) for v in vecs]
        for _ in range(2):
            x = [z[0] * u + jnp.dot(u.astype(BF16), r, preferred_element_type=F32)
                 for z, u, r in zip(z5, x, rb)]
        shifts = [jnp.transpose(jnp.broadcast_to(u[0:1] * i, (width, width)))
                  for u, i in zip(x, inv)]
        for (a, b), (z, r), shift, i in zip(groups, z5, shifts, inv):
            scale = math.sqrt(width - 1) * jnp.sqrt(i)
            weight = scale * jnp.where(eye, r + z, r) + shift
            wts[a, b] = weight
            wsend[a, b] = weight.astype(BF16)

    def w_copy(k, src, dst, dx, dy):
        return pltpu.make_async_remote_copy(
            src_ref=src, dst_ref=dst, send_sem=w_send.at[k], recv_sem=w_recv.at[k],
            device_id=at(dx, dy), device_id_type=MESH)

    def wx_copies():
        return [w_copy(0, wsend.at[na - 1], htx.at[0], 1, 0),
                w_copy(1, wsend.at[0], htx.at[1], -1, 0)]

    def wy_copies(k, first, count):
        rows = pl.ds(first, count)
        return [w_copy(k, wsend.at[rows, nbk - 1], hty.at[0, rows], 0, 1),
                w_copy(k + 1, wsend.at[rows, 0], hty.at[1, rows], 0, -1)]

    inner_wy = wy_copies(2, 2, na - 4)
    edge_wy = wy_copies(4, 0, 1) + wy_copies(6, na - 1, 1)
    last_wy = wy_copies(8, 1, 1) + wy_copies(10, na - 2, 1)
    inner = (na - 4) // 2

    def batch(i):
        h = i // inner
        r = i - inner * h
        one = (1 - h) * (2 + 2 * r) + h * r
        two = (1 - h) * (3 + 2 * r) + h * (na - 1 - r)
        return [(a, b) for a in (one, two) for b in range(nbk)]

    for k, group in enumerate(batch(0)):
        prepare(k, 0, group)
    for c in ys:
        c.wait_recv()
    total = jnp.sum(st_sum[...] + jnp.sum(st_y[...], axis=0), axis=1, keepdims=True)
    inflation = (width - 1) * total[1:2] / total[0:1]

    @pl.loop(0, inner + 2)
    def _(i):
        @pl.when(i == inner - 1)
        def _():
            for c in corner_copies():
                c.wait_recv()
            for k in range(HALO):
                for b in range(nbk + 2 * HALO):
                    grams[k, b] = landed[0, k, b]
                    grams[na + HALO + k, b] = landed[1, k, b]

        @pl.when(i == inner)
        def _():
            for c in inner_wy:
                c.start()

        transform(batch(i), i % 2, batch(i + 1 - (i + 1) // (inner + 2)))

        @pl.when(i == inner)
        def _():
            for c in wx_copies() + edge_wy:
                c.start()

    for c in last_wy:
        c.start()

    def blend(a, b, lower, upper):
        left = wts[a, b - 1] if b > 0 else hty[0, a].astype(F32)
        right = wts[a, b + 1] if b < nbk - 1 else hty[1, a].astype(F32)
        out[a, b] = ((4.0 * wts[a, b] + (upper + lower) + (left + right)) * 0.125).astype(BF16)

    @pl.loop(1, na - 1)
    def _(a):
        for b in range(1, nbk - 1):
            blend(a, b, wts[a - 1, b], wts[a + 1, b])

    def row_out(a):
        return pltpu.make_async_copy(out.at[a], out_h.at[a], o_sem.at[a])

    for c in inner_wy + last_wy:
        c.wait_recv()

    @pl.loop(1, na - 1)
    def _(a):
        for b in (0, nbk - 1):
            blend(a, b, wts[a - 1, b], wts[a + 1, b])
        row_out(a).start()

    for c in edge_wy + wx_copies():
        c.wait_recv()
    for b in range(nbk):
        blend(0, b, htx[0, b].astype(F32), wts[1, b])
        blend(na - 1, b, wts[na - 2, b], htx[1, b].astype(F32))
    row_out(0).start()
    row_out(na - 1).start()
    for i in range(na // 2):
        for c in ty_copies(i):
            c.wait_send()
    for c in tx_copies() + corner_copies() + xs + ys + wx_copies() + inner_wy + edge_wy + last_wy:
        c.wait_send()
    mean_out.wait()
    for a in range(na):
        row_out(a).wait()


def apply_weights(members_h, mean_th, blended_h, out_h, members, mean_t, blended, result, sem):
    na, nbk, levels, width = members.shape
    row = lax.broadcasted_iota(jnp.int32, (width, width), 0)

    def loads(a):
        return [pltpu.make_async_copy(src.at[a], dst.at[a], sem.at[k, a])
                for k, (src, dst) in enumerate(
                    [(blended_h, blended), (mean_th, mean_t), (members_h, members)])]

    def copy_out(a):
        return pltpu.make_async_copy(result.at[a], out_h.at[a], sem.at[3, a])

    for a in range(na):
        for c in loads(a):
            c.start()

    @pl.loop(0, na)
    def _(a):
        for c in loads(a):
            c.wait()
        for b in range(nbk):
            pick = jnp.where((row == b) | (row == b + nbk) | (row == b + 2 * nbk), 1.0, 0.0)
            left = jnp.concatenate([members[a, b], mean_t[a]], axis=1)
            right = jnp.concatenate([blended[a, b], pick.astype(BF16)], axis=0)
            result[a, b] = jnp.dot(left, right, preferred_element_type=F32).astype(BF16)
        copy_out(a).start()

    @pl.loop(0, na)
    def _(a):
        copy_out(a).wait()


def shards(nx, ny, members, mean_state, obs_pert, obs_rinv, innovation, obs_count, neighbours,
           loc_weight):
    na, nbk, slots, width = obs_pert.shape
    levels = members.shape[2]
    hbm = pl.BlockSpec(memory_space=pltpu.HBM)
    dma = pltpu.SemaphoreType.DMA
    half = width // 2
    blended, mean_t = pl.pallas_call(
        functools.partial(analysis_weights, nx, ny),
        out_shape=[
            jax.ShapeDtypeStruct((na, nbk, width, width), BF16),
            jax.ShapeDtypeStruct((na, levels, width), BF16),
        ],
        in_specs=[hbm] * 7,
        out_specs=[hbm] * 2,
        scratch_shapes=[
            pltpu.VMEM((na, nbk, width, width), BF16),
            pltpu.VMEM((na, levels, width), BF16),
            pltpu.SMEM((nbk, na), jnp.int32),
            pltpu.SMEM(neighbours.shape, jnp.int32),
            pltpu.SMEM(loc_weight.shape, F32),
            pltpu.VMEM(obs_pert.shape, BF16),
            pltpu.VMEM(obs_rinv.shape, BF16),
            pltpu.VMEM(innovation.shape, BF16),
            pltpu.VMEM(mean_state.shape, F32),
            pltpu.VMEM((na + 2 * HALO, nbk + 2 * HALO, half + 16, width), BF16),
            pltpu.VMEM((2, HALO, nbk + 2 * HALO, half + 16, width), BF16),
            pltpu.VMEM((2, 2 * nbk, width, width), F32),
            pltpu.VMEM((2, 2 * nbk, 8, width), F32),
            pltpu.VMEM((na, nbk, width, width), F32),
            pltpu.VMEM((na, nbk, width, width), BF16),
            pltpu.VMEM((2, nbk, width, width), BF16),
            pltpu.VMEM((2, na, width, width), BF16),
            pltpu.VMEM((8, slots), F32),
            pltpu.VMEM((nx - 1, 8, slots), F32),
            pltpu.VMEM((8, slots), F32),
            pltpu.VMEM((ny - 1, 8, slots), F32),
            dma((7,)), dma((na // 2,)), dma((na,)),
            dma((4 + na,)), dma((4 + na,)),
            dma((nx - 1,)), dma((nx - 1,)),
            dma((ny - 1,)), dma((ny - 1,)),
            dma((12,)), dma((12,)),
        ],
        compiler_params=pltpu.CompilerParams(
            collective_id=0, has_side_effects=True, vmem_limit_bytes=57 * 1024 * 1024),
    )(obs_count.T, neighbours, loc_weight, obs_pert, obs_rinv, innovation, mean_state)
    return pl.pallas_call(
        apply_weights,
        out_shape=jax.ShapeDtypeStruct(members.shape, BF16),
        in_specs=[hbm] * 3,
        out_specs=hbm,
        scratch_shapes=[
            pltpu.VMEM(members.shape, BF16),
            pltpu.VMEM((na, levels, width), BF16),
            pltpu.VMEM((na, nbk, width, width), BF16),
            pltpu.VMEM(members.shape, BF16),
            dma((4, na)),
        ],
        compiler_params=pltpu.CompilerParams(vmem_limit_bytes=57 * 1024 * 1024),
    )(members, mean_t, blended)


def solution(mesh):
    nx, ny = mesh.shape["tx"], mesh.shape["ty"]
    return jax.shard_map(
        functools.partial(shards, nx, ny),
        mesh=mesh,
        in_specs=(
            P("tx", "ty", None, None),
            P("tx", "ty", None),
            P("tx", "ty", None, None),
            P("tx", "ty", None),
            P("tx", "ty", None),
            P("tx", "ty"),
            P("tx", "ty", None),
            P("tx", "ty", None),
        ),
        out_specs=P("tx", "ty", None, None),
        check_vma=False,
    )
```

```python
import functools
import math

import jax
import jax.numpy as jnp
from jax import lax
from jax.experimental import pallas as pl
from jax.experimental.pallas import tpu as pltpu
from jax.sharding import PartitionSpec as P

MESH = pl.DeviceIdType.MESH
HALO = 2
F32 = jnp.float32
BF16 = jnp.bfloat16


def offsets(nx, ny):
    return [(dx, 0) for dx in range(1, nx)] + [(0, dy) for dy in range(1, ny)]


def matmul(a, b):
    return jnp.dot(a.astype(BF16), b.astype(BF16), preferred_element_type=F32)


def square(x):
    s, a = x
    return s * s, matmul(a, a) + (2.0 * s) * a


def product(left, right):
    s, a = left
    t, b = right
    return s * t, matmul(a, b) + (s * b + t * a)


def two_sweeps(y, beside):
    sq = [square(v) for v in y]
    beside()
    inner = [q[1] - 9.0 * v[1] for q, v in zip(sq, y)]
    cross = [matmul(q[1], i) for q, i in zip(sq, inner)]
    beside()
    out = []
    for c, q, v in zip(cross, sq, y):
        mid = q[0] - 9.0 * v[0] + 27.0
        out.append((q[0] * mid - 39.0 * v[0] + 36.0,
                    c + ((mid + q[0]) * q[1] - (9.0 * q[0] + 39.0) * v[1])))
    return out


def scaled_by(x, factor):
    return x[0] * factor, x[1] * factor


def analysis_weights(nx, ny, cnt_h, nb_h, lw_h, pert_h, rinv_h, innov_h, mean_h,
                     out_h, mean_th,
                     out, mean_t, cnt, nb, lw, pert, rinv, innov, mean,
                     grams, landed, ready, ready_v, wts, wsend, htx, hty, st_own, st_x, st_sum, st_y,
                     i_sem, p_sem, o_sem, g_send, g_recv, x_send, x_recv, y_send, y_recv,
                     w_send, w_recv):
    na, nbk, slots, width = pert.shape
    listed = nb.shape[2]
    half = width // 2
    mx, my = lax.axis_index("tx"), lax.axis_index("ty")

    def at(dx, dy):
        return {"tx": lax.rem(mx + (dx % nx), nx), "ty": lax.rem(my + (dy % ny), ny)}

    barrier = pltpu.get_barrier_semaphore()
    partners = offsets(nx, ny)
    for dx, dy in partners:
        pl.semaphore_signal(barrier, inc=1, device_id=at(dx, dy), device_id_type=MESH)

    def pair_at(i):
        h = i // 2
        return (1 - h) * (na - 2) * i + h * 2 * (i - 1)

    loads = [pltpu.make_async_copy(src, dst, i_sem.at[k]) for k, (src, dst) in enumerate([
        (cnt_h, cnt), (rinv_h, rinv), (innov_h, innov), (nb_h, nb), (lw_h, lw), (mean_h, mean)])]
    for c in loads[:3]:
        c.start()

    def pert_load(i):
        rows = pl.ds(pair_at(i), 2)
        return pltpu.make_async_copy(pert_h.at[rows], pert.at[rows], p_sem.at[i])

    for i in range(na // 2):
        pert_load(i).start()
    for c in loads[3:]:
        c.start()
    for c in loads[:3]:
        c.wait()

    lane = lax.broadcasted_iota(jnp.int32, (1, slots), 1)
    eye = (lax.broadcasted_iota(jnp.int32, (width, width), 0)
           == lax.broadcasted_iota(jnp.int32, (width, width), 1))
    hrow = lax.broadcasted_iota(jnp.int32, (half, width), 0)
    hlane = lax.broadcasted_iota(jnp.int32, (half, width), 1)
    sub = lax.broadcasted_iota(jnp.int32, (16, slots), 0)
    subw = lax.broadcasted_iota(jnp.int32, (16, width), 0)

    def gram_terms(blocks):
        ps = [pert[a, b] for a, b in blocks]
        lives = [lane < cnt[b, a] for a, b in blocks]
        qs = [jnp.where(live, rinv[a, b:b + 1, :].astype(F32), 0.0)
              for live, (a, b) in zip(lives, blocks)]
        ds = [innov[a, b:b + 1, :].astype(F32) for a, b in blocks]
        flipped = [jnp.transpose(p) for p in ps]
        scaled = [(f.astype(F32) * q).astype(BF16) for f, q in zip(flipped, qs)]
        qds = [q * d for q, d in zip(qs, ds)]
        his = [qd.astype(BF16).astype(F32) for qd in qds]
        tails = [jnp.where(sub == 0, hi, jnp.where(sub == 1, qd - hi, 0.0)).astype(BF16)
                 for hi, qd in zip(his, qds)]
        gs = [jnp.dot(x, p, preferred_element_type=F32) for x, p in zip(scaled, ps)]
        vs = [jnp.dot(x, p, preferred_element_type=F32) for x, p in zip(tails, ps)]
        diags = [jnp.sum(jnp.where(eye, g, 0.0), axis=0, keepdims=True) for g in gs]
        lowers = [pltpu.roll(g[half:], half, 1) for g in gs]
        packed = [jnp.where(hrow <= hlane, g[:half], lower) for g, lower in zip(gs, lowers)]
        first = second = 0.0
        for (a, b), pk, v, diag, qd, d, live in zip(blocks, packed, vs, diags, qds, ds, lives):
            vec = v[0:1] + v[1:2]
            vhi = vec.astype(BF16).astype(F32)
            extra = jnp.where(subw == 0, diag,
                              jnp.where(subw == 1, vhi, jnp.where(subw == 2, vec - vhi, 0.0)))
            grams[a + HALO, b + HALO, :half, :] = pk.astype(BF16)
            grams[a + HALO, b + HALO, half:, :] = extra.astype(BF16)
            first = first + qd * d
            second = second + (jnp.where(live, 1.0, 0.0) + diag * (1.0 / (width - 1)))
        return first, second

    def remote(src, dst, k, dx, dy):
        return pltpu.make_async_remote_copy(
            src_ref=src, dst_ref=dst, send_sem=g_send.at[k], recv_sem=g_recv.at[k],
            device_id=at(dx, dy), device_id_type=MESH)

    own_cols = pl.ds(HALO, nbk)
    ends = (pl.ds(0, HALO), pl.ds(nbk + HALO, HALO))

    def tx_copies():
        return [
            remote(grams.at[pl.ds(na, HALO), own_cols], landed.at[0, :, own_cols], 0, 1, 0),
            remote(grams.at[pl.ds(HALO, HALO), own_cols], landed.at[1, :, own_cols], 1, -1, 0)]

    def ty_copies(i):
        rows = pl.ds(HALO + pair_at(i), 2)
        k = 4 + 2 * i
        return [remote(grams.at[rows, pl.ds(nbk, HALO)], grams.at[rows, ends[0]], k, 0, 1),
                remote(grams.at[rows, pl.ds(HALO, HALO)], grams.at[rows, ends[1]], k + 1, 0, -1)]

    def corner_copies():
        return [remote(landed.at[:, :, pl.ds(nbk, HALO)], landed.at[:, :, ends[0]], 2, 0, 1),
                remote(landed.at[:, :, pl.ds(HALO, HALO)], landed.at[:, :, ends[1]], 3, 0, -1)]

    def gram_rows(i, sums):
        first, second = sums
        pert_load(i).wait()
        base = pair_at(i)
        one, two = gram_terms([(base + k, b) for k in range(2) for b in range(nbk)])

        @pl.when(i == 0)
        def _():
            pl.semaphore_wait(barrier, len(partners))
            tx_copies()[1].start()

        @pl.when(i == 1)
        def _():
            tx_copies()[0].start()

        for c in ty_copies(i):
            c.start()

        return first + one, second + two

    zero = jnp.zeros((1, slots), F32)
    sums = lax.fori_loop(0, na // 2, gram_rows, (zero, zero))
    rows8 = lax.broadcasted_iota(jnp.int32, (8, slots), 0)
    st_own[...] = jnp.where(rows8 == 0, sums[0], jnp.where(rows8 == 1, sums[1], 0.0))
    xs = [pltpu.make_async_remote_copy(
        src_ref=st_own, dst_ref=st_x.at[k - 1], send_sem=x_send.at[k - 1],
        recv_sem=x_recv.at[k - 1], device_id=at(k, 0), device_id_type=MESH)
        for k in range(1, nx)]
    for c in xs:
        c.start()

    loads[5].wait()

    row = jnp.concatenate([mean[a] for a in range(na)], axis=0)
    high = row.astype(BF16).astype(F32)
    rest = row - high
    middle = rest.astype(BF16).astype(F32)
    fill = jnp.zeros((width - 3 * na * nbk, row.shape[1]), F32)
    stack = jnp.concatenate([high, middle, rest - middle, fill], axis=0)
    mean_t[...] = jnp.transpose(stack).astype(BF16)
    mean_out = pltpu.make_async_copy(mean_t, mean_th, i_sem.at[6])
    mean_out.start()

    for c in xs:
        c.wait_recv()
    st_sum[...] = st_own[...] + jnp.sum(st_x[...], axis=0)
    ys = [pltpu.make_async_remote_copy(
        src_ref=st_sum, dst_ref=st_y.at[k - 1], send_sem=y_send.at[k - 1],
        recv_sem=y_recv.at[k - 1], device_id=at(0, k), device_id_type=MESH)
        for k in range(1, ny)]
    for c in ys:
        c.start()
    loads[3].wait()
    loads[4].wait()
    for c in tx_copies():
        c.wait_recv()
    for c in corner_copies():
        c.start()
    for i in range(na // 2):
        for c in ty_copies(i):
            c.wait_recv()

    def listed_sum(a, b):
        acc = None
        for j in range(listed):
            code = nb[a, b, j]
            down = lax.shift_right_logical(code * 13, 6)
            block = grams[a + down, b + (code - 5 * down)].astype(F32)
            term = lw[a, b, j] * block
            acc = term if acc is None else acc + term
        return acc

    def unpack(acc):
        c = acc[:half]
        diag = acc[half:half + 1]
        vec = acc[half + 1:half + 2] + acc[half + 2:half + 3]
        flipped = jnp.transpose(jnp.concatenate([c, c], axis=0))
        top = jnp.where(hrow <= hlane, c, flipped[:half])
        shifted = pltpu.roll(c, half, 1)
        column = hlane - half
        corner = jnp.where(hrow > column, shifted, jnp.where(hrow == column, diag, flipped[:half]))
        bottom = jnp.where(column < 0, flipped[half:], corner)
        return jnp.concatenate([top, bottom], axis=0), vec

    def total_of(m):
        return jnp.sum(jnp.sum(m, axis=0, keepdims=True), axis=1, keepdims=True)

    def prepare(k, slot, group):
        m, vec = unpack(listed_sum(*group))
        ready[slot, k] = m
        ready_v[slot, k] = jnp.broadcast_to(vec, (8, width))

    def transform(groups, slot, later):
        todo = list(enumerate(later))

        def beside():
            if todo:
                prepare(todo[0][0], 1 - slot, todo.pop(0)[1])

        ms = [ready[slot, k] for k in range(len(groups))]
        vecs = [ready_v[slot, k][0:1] for k in range(len(groups))]
        ms = [jnp.where(eye, m + inflation, m) for m in ms]
        inv = [lax.rsqrt(total_of(m * m)) for m in ms]
        mid = [total_of(jnp.where(eye, m, 0.0)) * (1.0 / width) for m in ms]
        y = [(c * i, jnp.where(eye, m - c, m) * i) for m, i, c in zip(ms, inv, mid)]
        z2 = two_sweeps(y, beside)
        v2 = [square(z) for z in z2]
        beside()
        t2 = [scaled_by(product(p, v), 1.0 / 256) for p, v in zip(y, v2)]
        beside()
        w = two_sweeps(t2, beside)
        z4 = [product(z, u) for z, u in zip(z2, w)]
        v4 = [square(u) for u in w]
        beside()
        t4 = [product(t, v) for t, v in zip(t2, v4)]
        beside()
        z5 = [(z[0] * (768.0 - t[0]), (768.0 - t[0]) * z[1] - z[0] * t[1] - matmul(z[1], t[1]))
              for z, t in zip(z4, t4)]
        while todo:
            beside()
        back = 1.0 / (256 * 512)
        z5 = [scaled_by(z, back) for z in z5]
        rb = [z[1].astype(BF16) for z in z5]
        x = [jnp.broadcast_to(v, (16, width)) for v in vecs]
        for _ in range(2):
            x = [z[0] * u + jnp.dot(u.astype(BF16), r, preferred_element_type=F32)
                 for z, u, r in zip(z5, x, rb)]
        shifts = [jnp.transpose(jnp.broadcast_to(u[0:1] * i, (width, width)))
                  for u, i in zip(x, inv)]
        for (a, b), (z, r), shift, i in zip(groups, z5, shifts, inv):
            scale = math.sqrt(width - 1) * jnp.sqrt(i)
            weight = scale * jnp.where(eye, r + z, r) + shift
            wts[a, b] = weight
            wsend[a, b] = weight.astype(BF16)

    def w_copy(k, src, dst, dx, dy):
        return pltpu.make_async_remote_copy(
            src_ref=src, dst_ref=dst, send_sem=w_send.at[k], recv_sem=w_recv.at[k],
            device_id=at(dx, dy), device_id_type=MESH)

    def wx_copies():
        return [w_copy(0, wsend.at[na - 1], htx.at[0], 1, 0),
                w_copy(1, wsend.at[0], htx.at[1], -1, 0)]

    def wy_copies(k, first, count):
        rows = pl.ds(first, count)
        return [w_copy(k, wsend.at[rows, nbk - 1], hty.at[0, rows], 0, 1),
                w_copy(k + 1, wsend.at[rows, 0], hty.at[1, rows], 0, -1)]

    inner_wy = wy_copies(2, 2, na - 4)
    edge_wy = wy_copies(4, 0, 1) + wy_copies(6, na - 1, 1)
    last_wy = wy_copies(8, 1, 1) + wy_copies(10, na - 2, 1)
    inner = (na - 4) // 2

    def batch(i):
        h = i // inner
        r = i - inner * h
        one = (1 - h) * (2 + 2 * r) + h * r
        two = (1 - h) * (3 + 2 * r) + h * (na - 1 - r)
        return [(a, b) for a in (one, two) for b in range(nbk)]

    for k, group in enumerate(batch(0)):
        prepare(k, 0, group)
    for c in ys:
        c.wait_recv()
    total = jnp.sum(st_sum[...] + jnp.sum(st_y[...], axis=0), axis=1, keepdims=True)
    inflation = (width - 1) * total[1:2] / total[0:1]

    @pl.loop(0, inner + 2)
    def _(i):
        @pl.when(i == inner - 1)
        def _():
            for c in corner_copies():
                c.wait_recv()
            for k in range(HALO):
                for b in range(nbk + 2 * HALO):
                    grams[k, b] = landed[0, k, b]
                    grams[na + HALO + k, b] = landed[1, k, b]

        @pl.when(i == inner)
        def _():
            for c in inner_wy:
                c.start()

        transform(batch(i), i % 2, batch(i + 1 - (i + 1) // (inner + 2)))

        @pl.when(i == inner)
        def _():
            for c in wx_copies() + edge_wy:
                c.start()

    for c in last_wy:
        c.start()

    def blend(a, b, lower, upper):
        left = wts[a, b - 1] if b > 0 else hty[0, a].astype(F32)
        right = wts[a, b + 1] if b < nbk - 1 else hty[1, a].astype(F32)
        out[a, b] = ((4.0 * wts[a, b] + (upper + lower) + (left + right)) * 0.125).astype(BF16)

    @pl.loop(1, na - 1)
    def _(a):
        for b in range(1, nbk - 1):
            blend(a, b, wts[a - 1, b], wts[a + 1, b])

    def row_out(a):
        return pltpu.make_async_copy(out.at[a], out_h.at[a], o_sem.at[a])

    for c in inner_wy + last_wy:
        c.wait_recv()

    @pl.loop(1, na - 1)
    def _(a):
        for b in (0, nbk - 1):
            blend(a, b, wts[a - 1, b], wts[a + 1, b])
        row_out(a).start()

    for c in edge_wy + wx_copies():
        c.wait_recv()
    for b in range(nbk):
        blend(0, b, htx[0, b].astype(F32), wts[1, b])
        blend(na - 1, b, wts[na - 2, b], htx[1, b].astype(F32))
    row_out(0).start()
    row_out(na - 1).start()
    for i in range(na // 2):
        for c in ty_copies(i):
            c.wait_send()
    for c in tx_copies() + corner_copies() + xs + ys + wx_copies() + inner_wy + edge_wy + last_wy:
        c.wait_send()
    mean_out.wait()
    for a in range(na):
        row_out(a).wait()


def apply_weights(members_h, mean_th, blended_h, out_h, members, mean_t, blended, result, sem):
    na, nbk, levels, width = members.shape
    row = lax.broadcasted_iota(jnp.int32, (width, width), 0)

    def loads(a):
        return [pltpu.make_async_copy(src.at[a], dst.at[a], sem.at[k, a])
                for k, (src, dst) in enumerate(
                    [(blended_h, blended), (members_h, members)])]

    def copy_out(a):
        return pltpu.make_async_copy(result.at[a], out_h.at[a], sem.at[3, a])

    mean_load = pltpu.make_async_copy(mean_th, mean_t, sem.at[2, 0])
    mean_load.start()
    for a in range(na):
        for c in loads(a):
            c.start()
    mean_load.wait()

    @pl.loop(0, na)
    def _(a):
        for c in loads(a):
            c.wait()
        for b in range(nbk):
            here = a * nbk + b
            pick = jnp.where((row == here) | (row == here + na * nbk) | (row == here + 2 * na * nbk),
                             1.0, 0.0)
            left = jnp.concatenate([members[a, b], mean_t[...]], axis=1)
            right = jnp.concatenate([blended[a, b], pick.astype(BF16)], axis=0)
            result[a, b] = jnp.dot(left, right, preferred_element_type=F32).astype(BF16)
        copy_out(a).start()

    @pl.loop(0, na)
    def _(a):
        copy_out(a).wait()


def shards(nx, ny, members, mean_state, obs_pert, obs_rinv, innovation, obs_count, neighbours,
           loc_weight):
    na, nbk, slots, width = obs_pert.shape
    levels = members.shape[2]
    hbm = pl.BlockSpec(memory_space=pltpu.HBM)
    dma = pltpu.SemaphoreType.DMA
    half = width // 2
    blended, mean_t = pl.pallas_call(
        functools.partial(analysis_weights, nx, ny),
        out_shape=[
            jax.ShapeDtypeStruct((na, nbk, width, width), BF16),
            jax.ShapeDtypeStruct((levels, width), BF16),
        ],
        in_specs=[hbm] * 7,
        out_specs=[hbm] * 2,
        scratch_shapes=[
            pltpu.VMEM((na, nbk, width, width), BF16),
            pltpu.VMEM((levels, width), BF16),
            pltpu.SMEM((nbk, na), jnp.int32),
            pltpu.SMEM(neighbours.shape, jnp.int32),
            pltpu.SMEM(loc_weight.shape, F32),
            pltpu.VMEM(obs_pert.shape, BF16),
            pltpu.VMEM(obs_rinv.shape, BF16),
            pltpu.VMEM(innovation.shape, BF16),
            pltpu.VMEM(mean_state.shape, F32),
            pltpu.VMEM((na + 2 * HALO, nbk + 2 * HALO, half + 16, width), BF16),
            pltpu.VMEM((2, HALO, nbk + 2 * HALO, half + 16, width), BF16),
            pltpu.VMEM((2, 2 * nbk, width, width), F32),
            pltpu.VMEM((2, 2 * nbk, 8, width), F32),
            pltpu.VMEM((na, nbk, width, width), F32),
            pltpu.VMEM((na, nbk, width, width), BF16),
            pltpu.VMEM((2, nbk, width, width), BF16),
            pltpu.VMEM((2, na, width, width), BF16),
            pltpu.VMEM((8, slots), F32),
            pltpu.VMEM((nx - 1, 8, slots), F32),
            pltpu.VMEM((8, slots), F32),
            pltpu.VMEM((ny - 1, 8, slots), F32),
            dma((7,)), dma((na // 2,)), dma((na,)),
            dma((4 + na,)), dma((4 + na,)),
            dma((nx - 1,)), dma((nx - 1,)),
            dma((ny - 1,)), dma((ny - 1,)),
            dma((12,)), dma((12,)),
        ],
        compiler_params=pltpu.CompilerParams(
            collective_id=0, has_side_effects=True, vmem_limit_bytes=57 * 1024 * 1024),
    )(obs_count.T, neighbours, loc_weight, obs_pert, obs_rinv, innovation, mean_state)
    return pl.pallas_call(
        apply_weights,
        out_shape=jax.ShapeDtypeStruct(members.shape, BF16),
        in_specs=[hbm] * 3,
        out_specs=hbm,
        scratch_shapes=[
            pltpu.VMEM(members.shape, BF16),
            pltpu.VMEM((levels, width), BF16),
            pltpu.VMEM((na, nbk, width, width), BF16),
            pltpu.VMEM(members.shape, BF16),
            dma((4, na)),
        ],
        compiler_params=pltpu.CompilerParams(vmem_limit_bytes=57 * 1024 * 1024),
    )(members, mean_t, blended)


def solution(mesh):
    nx, ny = mesh.shape["tx"], mesh.shape["ty"]
    return jax.shard_map(
        functools.partial(shards, nx, ny),
        mesh=mesh,
        in_specs=(
            P("tx", "ty", None, None),
            P("tx", "ty", None),
            P("tx", "ty", None, None),
            P("tx", "ty", None),
            P("tx", "ty", None),
            P("tx", "ty"),
            P("tx", "ty", None),
            P("tx", "ty", None),
        ),
        out_specs=P("tx", "ty", None, None),
        check_vma=False,
    )
```

```python
import functools
import math

import jax
import jax.numpy as jnp
from jax import lax
from jax.experimental import pallas as pl
from jax.experimental.pallas import tpu as pltpu
from jax.sharding import PartitionSpec as P

MESH = pl.DeviceIdType.MESH
HALO = 2
F32 = jnp.float32
BF16 = jnp.bfloat16


def offsets(nx, ny):
    return [(dx, 0) for dx in range(1, nx)] + [(0, dy) for dy in range(1, ny)]


def matmul(a, b):
    return jnp.dot(a.astype(BF16), b.astype(BF16), preferred_element_type=F32)


def square(x):
    s, a = x
    return s * s, matmul(a, a) + (2.0 * s) * a


def product(left, right):
    s, a = left
    t, b = right
    return s * t, matmul(a, b) + (s * b + t * a)


def two_sweeps(y, beside):
    sq = [square(v) for v in y]
    beside()
    inner = [q[1] - 9.0 * v[1] for q, v in zip(sq, y)]
    cross = [matmul(q[1], i) for q, i in zip(sq, inner)]
    beside()
    out = []
    for c, q, v in zip(cross, sq, y):
        mid = q[0] - 9.0 * v[0] + 27.0
        out.append((q[0] * mid - 39.0 * v[0] + 36.0,
                    c + ((mid + q[0]) * q[1] - (9.0 * q[0] + 39.0) * v[1])))
    return out


def scaled_by(x, factor):
    return x[0] * factor, x[1] * factor


def analysis_weights(nx, ny, cnt_h, nb_h, lw_h, pert_h, rinv_h, innov_h, mean_h,
                     out_h, mean_th,
                     out, mean_t, cnt, nb, lw, pert, rinv, innov, mean,
                     grams, landed, ready, ready_v, wts, wsend, htx, hty, st_own, st_x, st_sum, st_y,
                     i_sem, p_sem, o_sem, g_send, g_recv, x_send, x_recv, y_send, y_recv,
                     w_send, w_recv):
    na, nbk, slots, width = pert.shape
    listed = nb.shape[2]
    half = width // 2
    mx, my = lax.axis_index("tx"), lax.axis_index("ty")

    def at(dx, dy):
        return {"tx": lax.rem(mx + (dx % nx), nx), "ty": lax.rem(my + (dy % ny), ny)}

    barrier = pltpu.get_barrier_semaphore()
    partners = offsets(nx, ny)
    for dx, dy in partners:
        pl.semaphore_signal(barrier, inc=1, device_id=at(dx, dy), device_id_type=MESH)

    def pair_at(i):
        h = i // 2
        return (1 - h) * (na - 2) * i + h * 2 * (i - 1)

    loads = [pltpu.make_async_copy(src, dst, i_sem.at[k]) for k, (src, dst) in enumerate([
        (cnt_h, cnt), (rinv_h, rinv), (innov_h, innov), (nb_h, nb), (lw_h, lw), (mean_h, mean)])]
    for c in loads[:3]:
        c.start()

    def pert_load(i):
        rows = pl.ds(pair_at(i), 2)
        return pltpu.make_async_copy(pert_h.at[rows], pert.at[rows], p_sem.at[i])

    for i in range(na // 2):
        pert_load(i).start()
    for c in loads[3:]:
        c.start()
    for c in loads[:3]:
        c.wait()

    lane = lax.broadcasted_iota(jnp.int32, (1, slots), 1)
    eye = (lax.broadcasted_iota(jnp.int32, (width, width), 0)
           == lax.broadcasted_iota(jnp.int32, (width, width), 1))
    hrow = lax.broadcasted_iota(jnp.int32, (half, width), 0)
    hlane = lax.broadcasted_iota(jnp.int32, (half, width), 1)
    sub = lax.broadcasted_iota(jnp.int32, (16, slots), 0)
    subw = lax.broadcasted_iota(jnp.int32, (16, width), 0)

    def gram_terms(blocks):
        ps = [pert[a, b] for a, b in blocks]
        lives = [lane < cnt[b, a] for a, b in blocks]
        qs = [jnp.where(live, rinv[a, b:b + 1, :].astype(F32), 0.0)
              for live, (a, b) in zip(lives, blocks)]
        ds = [innov[a, b:b + 1, :].astype(F32) for a, b in blocks]
        flipped = [jnp.transpose(p) for p in ps]
        scaled = [(f.astype(F32) * q).astype(BF16) for f, q in zip(flipped, qs)]
        qds = [q * d for q, d in zip(qs, ds)]
        his = [qd.astype(BF16).astype(F32) for qd in qds]
        tails = [jnp.where(sub == 0, hi, jnp.where(sub == 1, qd - hi, 0.0)).astype(BF16)
                 for hi, qd in zip(his, qds)]
        gs = [jnp.dot(x, p, preferred_element_type=F32) for x, p in zip(scaled, ps)]
        vs = [jnp.dot(x, p, preferred_element_type=F32) for x, p in zip(tails, ps)]
        diags = [jnp.sum(jnp.where(eye, g, 0.0), axis=0, keepdims=True) for g in gs]
        lowers = [pltpu.roll(g[half:], half, 1) for g in gs]
        packed = [jnp.where(hrow <= hlane, g[:half], lower) for g, lower in zip(gs, lowers)]
        first = second = 0.0
        for (a, b), pk, v, diag, qd, d, live in zip(blocks, packed, vs, diags, qds, ds, lives):
            vec = v[0:1] + v[1:2]
            vhi = vec.astype(BF16).astype(F32)
            extra = jnp.where(subw == 0, diag,
                              jnp.where(subw == 1, vhi, jnp.where(subw == 2, vec - vhi, 0.0)))
            grams[a + HALO, b + HALO, :half, :] = pk.astype(BF16)
            grams[a + HALO, b + HALO, half:, :] = extra.astype(BF16)
            first = first + qd * d
            second = second + (jnp.where(live, 1.0, 0.0) + diag * (1.0 / (width - 1)))
        return first, second

    def remote(src, dst, k, dx, dy):
        return pltpu.make_async_remote_copy(
            src_ref=src, dst_ref=dst, send_sem=g_send.at[k], recv_sem=g_recv.at[k],
            device_id=at(dx, dy), device_id_type=MESH)

    own_cols = pl.ds(HALO, nbk)
    ends = (pl.ds(0, HALO), pl.ds(nbk + HALO, HALO))

    def tx_copies():
        return [
            remote(grams.at[pl.ds(na, HALO), own_cols], landed.at[0, :, own_cols], 0, 1, 0),
            remote(grams.at[pl.ds(HALO, HALO), own_cols], landed.at[1, :, own_cols], 1, -1, 0)]

    def ty_copies(i):
        rows = pl.ds(HALO + pair_at(i), 2)
        k = 4 + 2 * i
        return [remote(grams.at[rows, pl.ds(nbk, HALO)], grams.at[rows, ends[0]], k, 0, 1),
                remote(grams.at[rows, pl.ds(HALO, HALO)], grams.at[rows, ends[1]], k + 1, 0, -1)]

    def corner_copies():
        return [remote(landed.at[:, :, pl.ds(nbk, HALO)], landed.at[:, :, ends[0]], 2, 0, 1),
                remote(landed.at[:, :, pl.ds(HALO, HALO)], landed.at[:, :, ends[1]], 3, 0, -1)]

    def gram_rows(i, sums):
        first, second = sums
        pert_load(i).wait()
        base = pair_at(i)
        one, two = gram_terms([(base + k, b) for k in range(2) for b in range(nbk)])

        @pl.when(i == 1)
        def _():
            pl.semaphore_wait(barrier, len(partners))
            for c in ty_copies(0) + tx_copies():
                c.start()

        @pl.when(i >= 1)
        def _():
            for c in ty_copies(i):
                c.start()

        return first + one, second + two

    zero = jnp.zeros((1, slots), F32)
    sums = lax.fori_loop(0, na // 2, gram_rows, (zero, zero))
    rows8 = lax.broadcasted_iota(jnp.int32, (8, slots), 0)
    st_own[...] = jnp.where(rows8 == 0, sums[0], jnp.where(rows8 == 1, sums[1], 0.0))
    xs = [pltpu.make_async_remote_copy(
        src_ref=st_own, dst_ref=st_x.at[k - 1], send_sem=x_send.at[k - 1],
        recv_sem=x_recv.at[k - 1], device_id=at(k, 0), device_id_type=MESH)
        for k in range(1, nx)]
    for c in xs:
        c.start()

    loads[5].wait()

    @pl.loop(0, na)
    def _(a):
        row = mean[a]
        high = row.astype(BF16).astype(F32)
        rest = row - high
        middle = rest.astype(BF16).astype(F32)
        fill = jnp.zeros((width - 3 * nbk, row.shape[1]), F32)
        stack = jnp.concatenate([high, middle, rest - middle, fill], axis=0)
        mean_t[a] = jnp.transpose(stack).astype(BF16)

    mean_out = pltpu.make_async_copy(mean_t, mean_th, i_sem.at[6])
    mean_out.start()

    for c in xs:
        c.wait_recv()
    st_sum[...] = st_own[...] + jnp.sum(st_x[...], axis=0)
    ys = [pltpu.make_async_remote_copy(
        src_ref=st_sum, dst_ref=st_y.at[k - 1], send_sem=y_send.at[k - 1],
        recv_sem=y_recv.at[k - 1], device_id=at(0, k), device_id_type=MESH)
        for k in range(1, ny)]
    for c in ys:
        c.start()
    loads[3].wait()
    loads[4].wait()
    for i in range(na // 2):
        for c in ty_copies(i):
            c.wait_recv()
    for c in tx_copies():
        c.wait_recv()
    for c in corner_copies():
        c.start()

    def listed_sum(a, b):
        acc = None
        for j in range(listed):
            code = nb[a, b, j]
            down = lax.shift_right_logical(code * 13, 6)
            block = grams[a + down, b + (code - 5 * down)].astype(F32)
            term = lw[a, b, j] * block
            acc = term if acc is None else acc + term
        return acc

    def unpack(acc):
        c = acc[:half]
        diag = acc[half:half + 1]
        vec = acc[half + 1:half + 2] + acc[half + 2:half + 3]
        flipped = jnp.transpose(jnp.concatenate([c, c], axis=0))
        top = jnp.where(hrow <= hlane, c, flipped[:half])
        shifted = pltpu.roll(c, half, 1)
        column = hlane - half
        corner = jnp.where(hrow > column, shifted, jnp.where(hrow == column, diag, flipped[:half]))
        bottom = jnp.where(column < 0, flipped[half:], corner)
        return jnp.concatenate([top, bottom], axis=0), vec

    def total_of(m):
        return jnp.sum(jnp.sum(m, axis=0, keepdims=True), axis=1, keepdims=True)

    def prepare(k, slot, group):
        m, vec = unpack(listed_sum(*group))
        ready[slot, k] = m
        ready_v[slot, k] = jnp.broadcast_to(vec, (8, width))

    def transform(groups, slot, later):
        todo = list(enumerate(later))

        def beside():
            if todo:
                prepare(todo[0][0], 1 - slot, todo.pop(0)[1])

        ms = [ready[slot, k] for k in range(len(groups))]
        vecs = [ready_v[slot, k][0:1] for k in range(len(groups))]
        ms = [jnp.where(eye, m + inflation, m) for m in ms]
        inv = [lax.rsqrt(total_of(m * m)) for m in ms]
        mid = [total_of(jnp.where(eye, m, 0.0)) * (1.0 / width) for m in ms]
        y = [(c * i, jnp.where(eye, m - c, m) * i) for m, i, c in zip(ms, inv, mid)]
        z2 = two_sweeps(y, beside)
        v2 = [square(z) for z in z2]
        beside()
        t2 = [scaled_by(product(p, v), 1.0 / 256) for p, v in zip(y, v2)]
        beside()
        w = two_sweeps(t2, beside)
        z4 = [product(z, u) for z, u in zip(z2, w)]
        v4 = [square(u) for u in w]
        beside()
        t4 = [product(t, v) for t, v in zip(t2, v4)]
        beside()
        z5 = [(z[0] * (768.0 - t[0]), (768.0 - t[0]) * z[1] - z[0] * t[1] - matmul(z[1], t[1]))
              for z, t in zip(z4, t4)]
        while todo:
            beside()
        back = 1.0 / (256 * 512)
        z5 = [scaled_by(z, back) for z in z5]
        rb = [z[1].astype(BF16) for z in z5]
        x = [jnp.broadcast_to(v, (16, width)) for v in vecs]
        for _ in range(2):
            x = [z[0] * u + jnp.dot(u.astype(BF16), r, preferred_element_type=F32)
                 for z, u, r in zip(z5, x, rb)]
        shifts = [jnp.transpose(jnp.broadcast_to(u[0:1] * i, (width, width)))
                  for u, i in zip(x, inv)]
        for (a, b), (z, r), shift, i in zip(groups, z5, shifts, inv):
            scale = math.sqrt(width - 1) * jnp.sqrt(i)
            weight = scale * jnp.where(eye, r + z, r) + shift
            wts[a, b] = weight
            wsend[a, b] = weight.astype(BF16)

    def w_copy(k, src, dst, dx, dy):
        return pltpu.make_async_remote_copy(
            src_ref=src, dst_ref=dst, send_sem=w_send.at[k], recv_sem=w_recv.at[k],
            device_id=at(dx, dy), device_id_type=MESH)

    def wx_copies():
        return [w_copy(0, wsend.at[na - 1], htx.at[0], 1, 0),
                w_copy(1, wsend.at[0], htx.at[1], -1, 0)]

    def wy_copies(k, first, count):
        rows = pl.ds(first, count)
        return [w_copy(k, wsend.at[rows, nbk - 1], hty.at[0, rows], 0, 1),
                w_copy(k + 1, wsend.at[rows, 0], hty.at[1, rows], 0, -1)]

    inner_wy = wy_copies(2, 2, na - 4)
    edge_wy = wy_copies(4, 0, 1) + wy_copies(6, na - 1, 1)
    last_wy = wy_copies(8, 1, 1) + wy_copies(10, na - 2, 1)
    inner = (na - 4) // 2

    def batch(i):
        h = i // inner
        r = i - inner * h
        one = (1 - h) * (2 + 2 * r) + h * r
        two = (1 - h) * (3 + 2 * r) + h * (na - 1 - r)
        return [(a, b) for a in (one, two) for b in range(nbk)]

    for k, group in enumerate(batch(0)):
        prepare(k, 0, group)
    for c in ys:
        c.wait_recv()
    total = jnp.sum(st_sum[...] + jnp.sum(st_y[...], axis=0), axis=1, keepdims=True)
    inflation = (width - 1) * total[1:2] / total[0:1]

    @pl.loop(0, inner + 2)
    def _(i):
        @pl.when(i == inner - 1)
        def _():
            for c in corner_copies():
                c.wait_recv()
            for k in range(HALO):
                for b in range(nbk + 2 * HALO):
                    grams[k, b] = landed[0, k, b]
                    grams[na + HALO + k, b] = landed[1, k, b]

        @pl.when(i == inner)
        def _():
            for c in inner_wy:
                c.start()

        transform(batch(i), i % 2, batch(i + 1 - (i + 1) // (inner + 2)))

        @pl.when(i == inner)
        def _():
            for c in wx_copies() + edge_wy:
                c.start()

    for c in last_wy:
        c.start()

    def blend(a, b, lower, upper):
        left = wts[a, b - 1] if b > 0 else hty[0, a].astype(F32)
        right = wts[a, b + 1] if b < nbk - 1 else hty[1, a].astype(F32)
        out[a, b] = ((4.0 * wts[a, b] + (upper + lower) + (left + right)) * 0.125).astype(BF16)

    @pl.loop(1, na - 1)
    def _(a):
        for b in range(1, nbk - 1):
            blend(a, b, wts[a - 1, b], wts[a + 1, b])

    def row_out(a):
        return pltpu.make_async_copy(out.at[a], out_h.at[a], o_sem.at[a])

    for c in inner_wy + last_wy:
        c.wait_recv()

    @pl.loop(1, na - 1)
    def _(a):
        for b in (0, nbk - 1):
            blend(a, b, wts[a - 1, b], wts[a + 1, b])
        row_out(a).start()

    for c in edge_wy + wx_copies():
        c.wait_recv()
    for b in range(nbk):
        blend(0, b, htx[0, b].astype(F32), wts[1, b])
        blend(na - 1, b, wts[na - 2, b], htx[1, b].astype(F32))
    row_out(0).start()
    row_out(na - 1).start()
    for i in range(na // 2):
        for c in ty_copies(i):
            c.wait_send()
    for c in tx_copies() + corner_copies() + xs + ys + wx_copies() + inner_wy + edge_wy + last_wy:
        c.wait_send()
    mean_out.wait()
    for a in range(na):
        row_out(a).wait()


def apply_weights(members_h, mean_th, blended_h, out_h, members, mean_t, blended, result, sem):
    na, nbk, levels, width = members.shape
    row = lax.broadcasted_iota(jnp.int32, (width, width), 0)

    def loads(a):
        return [pltpu.make_async_copy(src.at[a], dst.at[a], sem.at[k, a])
                for k, (src, dst) in enumerate(
                    [(blended_h, blended), (mean_th, mean_t), (members_h, members)])]

    def copy_out(a):
        return pltpu.make_async_copy(result.at[a], out_h.at[a], sem.at[3, a])

    for a in range(na):
        for c in loads(a):
            c.start()

    picks = [jnp.where((row == b) | (row == b + nbk) | (row == b + 2 * nbk), 1.0, 0.0).astype(BF16)
             for b in range(nbk)]

    @pl.loop(0, na // 2)
    def _(i):
        pair = (2 * i, 2 * i + 1)
        for a in pair:
            for c in loads(a):
                c.wait()
        groups = [(a, b) for a in pair for b in range(nbk)]
        lefts = [jnp.concatenate([members[a, b], mean_t[a]], axis=1) for a, b in groups]
        rights = [jnp.concatenate([blended[a, b], picks[b]], axis=0) for a, b in groups]
        values = [jnp.dot(x, y, preferred_element_type=F32) for x, y in zip(lefts, rights)]
        for (a, b), value in zip(groups, values):
            result[a, b] = value.astype(BF16)
        for a in pair:
            copy_out(a).start()

    @pl.loop(0, na)
    def _(a):
        copy_out(a).wait()


def shards(nx, ny, members, mean_state, obs_pert, obs_rinv, innovation, obs_count, neighbours,
           loc_weight):
    na, nbk, slots, width = obs_pert.shape
    levels = members.shape[2]
    hbm = pl.BlockSpec(memory_space=pltpu.HBM)
    dma = pltpu.SemaphoreType.DMA
    half = width // 2
    blended, mean_t = pl.pallas_call(
        functools.partial(analysis_weights, nx, ny),
        out_shape=[
            jax.ShapeDtypeStruct((na, nbk, width, width), BF16),
            jax.ShapeDtypeStruct((na, levels, width), BF16),
        ],
        in_specs=[hbm] * 7,
        out_specs=[hbm] * 2,
        scratch_shapes=[
            pltpu.VMEM((na, nbk, width, width), BF16),
            pltpu.VMEM((na, levels, width), BF16),
            pltpu.SMEM((nbk, na), jnp.int32),
            pltpu.SMEM(neighbours.shape, jnp.int32),
            pltpu.SMEM(loc_weight.shape, F32),
            pltpu.VMEM(obs_pert.shape, BF16),
            pltpu.VMEM(obs_rinv.shape, BF16),
            pltpu.VMEM(innovation.shape, BF16),
            pltpu.VMEM(mean_state.shape, F32),
            pltpu.VMEM((na + 2 * HALO, nbk + 2 * HALO, half + 16, width), BF16),
            pltpu.VMEM((2, HALO, nbk + 2 * HALO, half + 16, width), BF16),
            pltpu.VMEM((2, 2 * nbk, width, width), F32),
            pltpu.VMEM((2, 2 * nbk, 8, width), F32),
            pltpu.VMEM((na, nbk, width, width), F32),
            pltpu.VMEM((na, nbk, width, width), BF16),
            pltpu.VMEM((2, nbk, width, width), BF16),
            pltpu.VMEM((2, na, width, width), BF16),
            pltpu.VMEM((8, slots), F32),
            pltpu.VMEM((nx - 1, 8, slots), F32),
            pltpu.VMEM((8, slots), F32),
            pltpu.VMEM((ny - 1, 8, slots), F32),
            dma((7,)), dma((na // 2,)), dma((na,)),
            dma((4 + na,)), dma((4 + na,)),
            dma((nx - 1,)), dma((nx - 1,)),
            dma((ny - 1,)), dma((ny - 1,)),
            dma((12,)), dma((12,)),
        ],
        compiler_params=pltpu.CompilerParams(
            collective_id=0, has_side_effects=True, vmem_limit_bytes=57 * 1024 * 1024),
    )(obs_count.T, neighbours, loc_weight, obs_pert, obs_rinv, innovation, mean_state)
    return pl.pallas_call(
        apply_weights,
        out_shape=jax.ShapeDtypeStruct(members.shape, BF16),
        in_specs=[hbm] * 3,
        out_specs=hbm,
        scratch_shapes=[
            pltpu.VMEM(members.shape, BF16),
            pltpu.VMEM((na, levels, width), BF16),
            pltpu.VMEM((na, nbk, width, width), BF16),
            pltpu.VMEM(members.shape, BF16),
            dma((4, na)),
        ],
        compiler_params=pltpu.CompilerParams(vmem_limit_bytes=57 * 1024 * 1024),
    )(members, mean_t, blended)


def solution(mesh):
    nx, ny = mesh.shape["tx"], mesh.shape["ty"]
    return jax.shard_map(
        functools.partial(shards, nx, ny),
        mesh=mesh,
        in_specs=(
            P("tx", "ty", None, None),
            P("tx", "ty", None),
            P("tx", "ty", None, None),
            P("tx", "ty", None),
            P("tx", "ty", None),
            P("tx", "ty"),
            P("tx", "ty", None),
            P("tx", "ty", None),
        ),
        out_specs=P("tx", "ty", None, None),
        check_vma=False,
    )
```

```python
import functools
import math

import jax
import jax.numpy as jnp
from jax import lax
from jax.experimental import pallas as pl
from jax.experimental.pallas import tpu as pltpu
from jax.sharding import PartitionSpec as P

MESH = pl.DeviceIdType.MESH
HALO = 2
F32 = jnp.float32
BF16 = jnp.bfloat16


def offsets(nx, ny):
    return [(dx, 0) for dx in range(1, nx)] + [(0, dy) for dy in range(1, ny)]


def matmul(a, b):
    return jnp.dot(a.astype(BF16), b.astype(BF16), preferred_element_type=F32)


def square(x):
    s, a = x
    return s * s, matmul(a, a) + (2.0 * s) * a


def product(left, right):
    s, a = left
    t, b = right
    return s * t, matmul(a, b) + (s * b + t * a)


def two_sweeps(y, beside):
    sq = [square(v) for v in y]
    beside()
    inner = [q[1] - 9.0 * v[1] for q, v in zip(sq, y)]
    cross = [matmul(q[1], i) for q, i in zip(sq, inner)]
    beside()
    out = []
    for c, q, v in zip(cross, sq, y):
        mid = q[0] - 9.0 * v[0] + 27.0
        out.append((q[0] * mid - 39.0 * v[0] + 36.0,
                    c + ((mid + q[0]) * q[1] - (9.0 * q[0] + 39.0) * v[1])))
    return out


def scaled_by(x, factor):
    return x[0] * factor, x[1] * factor


def analysis_weights(nx, ny, cnt_h, nb_h, lw_h, pert_h, rinv_h, innov_h, mean_h,
                     out_h, mean_th,
                     out, mean_t, cnt, nb, lw, pert, rinv, innov, mean,
                     grams, landed, ready, ready_v, wts, wsend, htx, hty, st_own, st_x, st_sum, st_y,
                     i_sem, p_sem, o_sem, g_send, g_recv, x_send, x_recv, y_send, y_recv,
                     w_send, w_recv):
    na, nbk, slots, width = pert.shape
    listed = nb.shape[2]
    half = width // 2
    mx, my = lax.axis_index("tx"), lax.axis_index("ty")

    def at(dx, dy):
        return {"tx": lax.rem(mx + (dx % nx), nx), "ty": lax.rem(my + (dy % ny), ny)}

    barrier = pltpu.get_barrier_semaphore()
    partners = offsets(nx, ny)
    for dx, dy in partners:
        pl.semaphore_signal(barrier, inc=1, device_id=at(dx, dy), device_id_type=MESH)

    def pair_at(i):
        h = i // 2
        return (1 - h) * (na - 2) * i + h * 2 * (i - 1)

    loads = [pltpu.make_async_copy(src, dst, i_sem.at[k]) for k, (src, dst) in enumerate([
        (cnt_h, cnt), (rinv_h, rinv), (innov_h, innov), (nb_h, nb), (lw_h, lw), (mean_h, mean)])]
    for c in loads[:3]:
        c.start()

    def pert_load(i):
        rows = pl.ds(pair_at(i), 2)
        return pltpu.make_async_copy(pert_h.at[rows], pert.at[rows], p_sem.at[i])

    for i in range(na // 2):
        pert_load(i).start()
    for c in loads[3:]:
        c.start()
    for c in loads[:3]:
        c.wait()

    lane = lax.broadcasted_iota(jnp.int32, (1, slots), 1)
    eye = (lax.broadcasted_iota(jnp.int32, (width, width), 0)
           == lax.broadcasted_iota(jnp.int32, (width, width), 1))
    hrow = lax.broadcasted_iota(jnp.int32, (half, width), 0)
    hlane = lax.broadcasted_iota(jnp.int32, (half, width), 1)
    sub = lax.broadcasted_iota(jnp.int32, (16, slots), 0)
    subw = lax.broadcasted_iota(jnp.int32, (16, width), 0)

    def gram_terms(blocks):
        ps = [pert[a, b] for a, b in blocks]
        lives = [lane < cnt[b, a] for a, b in blocks]
        qs = [jnp.where(live, rinv[a, b:b + 1, :].astype(F32), 0.0)
              for live, (a, b) in zip(lives, blocks)]
        ds = [innov[a, b:b + 1, :].astype(F32) for a, b in blocks]
        flipped = [jnp.transpose(p) for p in ps]
        scaled = [(f.astype(F32) * q).astype(BF16) for f, q in zip(flipped, qs)]
        qds = [q * d for q, d in zip(qs, ds)]
        his = [qd.astype(BF16).astype(F32) for qd in qds]
        tails = [jnp.where(sub == 0, hi, jnp.where(sub == 1, qd - hi, 0.0)).astype(BF16)
                 for hi, qd in zip(his, qds)]
        gs = [jnp.dot(x, p, preferred_element_type=F32) for x, p in zip(scaled, ps)]
        vs = [jnp.dot(x, p, preferred_element_type=F32) for x, p in zip(tails, ps)]
        diags = [jnp.sum(jnp.where(eye, g, 0.0), axis=0, keepdims=True) for g in gs]
        lowers = [pltpu.roll(g[half:], half, 1) for g in gs]
        packed = [jnp.where(hrow <= hlane, g[:half], lower) for g, lower in zip(gs, lowers)]
        first = second = 0.0
        for (a, b), pk, v, diag, qd, d, live in zip(blocks, packed, vs, diags, qds, ds, lives):
            vec = v[0:1] + v[1:2]
            vhi = vec.astype(BF16).astype(F32)
            extra = jnp.where(subw == 0, diag,
                              jnp.where(subw == 1, vhi, jnp.where(subw == 2, vec - vhi, 0.0)))
            grams[a + HALO, b + HALO, :half, :] = pk.astype(BF16)
            grams[a + HALO, b + HALO, half:, :] = extra.astype(BF16)
            first = first + qd * d
            second = second + (jnp.where(live, 1.0, 0.0) + diag * (1.0 / (width - 1)))
        return first, second

    def remote(src, dst, k, dx, dy):
        return pltpu.make_async_remote_copy(
            src_ref=src, dst_ref=dst, send_sem=g_send.at[k], recv_sem=g_recv.at[k],
            device_id=at(dx, dy), device_id_type=MESH)

    own_cols = pl.ds(HALO, nbk)
    ends = (pl.ds(0, HALO), pl.ds(nbk + HALO, HALO))

    def tx_copies():
        return [
            remote(grams.at[pl.ds(na, HALO), own_cols], landed.at[0, :, own_cols], 0, 1, 0),
            remote(grams.at[pl.ds(HALO, HALO), own_cols], landed.at[1, :, own_cols], 1, -1, 0)]

    def ty_copies(i):
        rows = pl.ds(HALO + pair_at(i), 2)
        k = 4 + 2 * i
        return [remote(grams.at[rows, pl.ds(nbk, HALO)], grams.at[rows, ends[0]], k, 0, 1),
                remote(grams.at[rows, pl.ds(HALO, HALO)], grams.at[rows, ends[1]], k + 1, 0, -1)]

    def corner_copies():
        return [remote(landed.at[:, :, pl.ds(nbk, HALO)], landed.at[:, :, ends[0]], 2, 0, 1),
                remote(landed.at[:, :, pl.ds(HALO, HALO)], landed.at[:, :, ends[1]], 3, 0, -1)]

    def gram_rows(i, sums):
        first, second = sums
        pert_load(i).wait()
        base = pair_at(i)
        one, two = gram_terms([(base + k, b) for k in range(2) for b in range(nbk)])

        @pl.when(i == 1)
        def _():
            pl.semaphore_wait(barrier, len(partners))
            for c in ty_copies(0) + tx_copies():
                c.start()

        @pl.when(i >= 1)
        def _():
            for c in ty_copies(i):
                c.start()

        return first + one, second + two

    zero = jnp.zeros((1, slots), F32)
    sums = lax.fori_loop(0, na // 2, gram_rows, (zero, zero))
    rows8 = lax.broadcasted_iota(jnp.int32, (8, slots), 0)
    st_own[...] = jnp.where(rows8 == 0, sums[0], jnp.where(rows8 == 1, sums[1], 0.0))
    xs = [pltpu.make_async_remote_copy(
        src_ref=st_own, dst_ref=st_x.at[k - 1], send_sem=x_send.at[k - 1],
        recv_sem=x_recv.at[k - 1], device_id=at(k, 0), device_id_type=MESH)
        for k in range(1, nx)]
    for c in xs:
        c.start()

    loads[5].wait()

    @pl.loop(0, na)
    def _(a):
        row = mean[a]
        high = row.astype(BF16).astype(F32)
        rest = row - high
        middle = rest.astype(BF16).astype(F32)
        fill = jnp.zeros((width - 3 * nbk, row.shape[1]), F32)
        stack = jnp.concatenate([high, middle, rest - middle, fill], axis=0)
        mean_t[a] = jnp.transpose(stack).astype(BF16)

    mean_out = pltpu.make_async_copy(mean_t, mean_th, i_sem.at[6])
    mean_out.start()

    for c in xs:
        c.wait_recv()
    st_sum[...] = st_own[...] + jnp.sum(st_x[...], axis=0)
    ys = [pltpu.make_async_remote_copy(
        src_ref=st_sum, dst_ref=st_y.at[k - 1], send_sem=y_send.at[k - 1],
        recv_sem=y_recv.at[k - 1], device_id=at(0, k), device_id_type=MESH)
        for k in range(1, ny)]
    for c in ys:
        c.start()
    loads[3].wait()
    loads[4].wait()
    for i in range(na // 2):
        for c in ty_copies(i):
            c.wait_recv()
    for c in tx_copies():
        c.wait_recv()
    for c in corner_copies():
        c.start()

    def listed_sum(a, b):
        acc = None
        for j in range(listed):
            code = nb[a, b, j]
            down = lax.shift_right_logical(code * 13, 6)
            block = grams[a + down, b + (code - 5 * down)].astype(F32)
            term = lw[a, b, j] * block
            acc = term if acc is None else acc + term
        return acc

    def unpack(acc):
        c = acc[:half]
        diag = acc[half:half + 1]
        vec = acc[half + 1:half + 2] + acc[half + 2:half + 3]
        flipped = jnp.transpose(jnp.concatenate([c, c], axis=0))
        top = jnp.where(hrow <= hlane, c, flipped[:half])
        shifted = pltpu.roll(c, half, 1)
        column = hlane - half
        corner = jnp.where(hrow > column, shifted, jnp.where(hrow == column, diag, flipped[:half]))
        bottom = jnp.where(column < 0, flipped[half:], corner)
        return jnp.concatenate([top, bottom], axis=0), vec

    def total_of(m):
        return jnp.sum(jnp.sum(m, axis=0, keepdims=True), axis=1, keepdims=True)

    def prepare(k, slot, group):
        m, vec = unpack(listed_sum(*group))
        ready[slot, k] = m
        ready_v[slot, k] = jnp.broadcast_to(vec, (8, width))

    def transform(groups, slot, later):
        todo = list(enumerate(later))

        def beside():
            if todo:
                prepare(todo[0][0], 1 - slot, todo.pop(0)[1])

        ms = [ready[slot, k] for k in range(len(groups))]
        vecs = [ready_v[slot, k][0:1] for k in range(len(groups))]
        ms = [jnp.where(eye, m + inflation, m) for m in ms]
        inv = [lax.rsqrt(total_of(m * m)) for m in ms]
        mid = [total_of(jnp.where(eye, m, 0.0)) * (1.0 / width) for m in ms]
        y = [(c * i, jnp.where(eye, m - c, m) * i) for m, i, c in zip(ms, inv, mid)]
        z2 = two_sweeps(y, beside)
        v2 = [square(z) for z in z2]
        beside()
        t2 = [scaled_by(product(p, v), 1.0 / 256) for p, v in zip(y, v2)]
        beside()
        w = two_sweeps(t2, beside)
        z4 = [product(z, u) for z, u in zip(z2, w)]
        v4 = [square(u) for u in w]
        beside()
        t4 = [product(t, v) for t, v in zip(t2, v4)]
        beside()
        z5 = [(z[0] * (768.0 - t[0]), (768.0 - t[0]) * z[1] - z[0] * t[1] - matmul(z[1], t[1]))
              for z, t in zip(z4, t4)]
        while todo:
            beside()
        back = 1.0 / (256 * 512)
        z5 = [scaled_by(z, back) for z in z5]
        rb = [z[1].astype(BF16) for z in z5]
        x = [jnp.broadcast_to(v, (16, width)) for v in vecs]
        for _ in range(2):
            x = [z[0] * u + jnp.dot(u.astype(BF16), r, preferred_element_type=F32)
                 for z, u, r in zip(z5, x, rb)]
        shifts = [jnp.transpose(jnp.broadcast_to(u[0:1] * i, (width, width)))
                  for u, i in zip(x, inv)]
        for (a, b), (z, r), shift, i in zip(groups, z5, shifts, inv):
            scale = math.sqrt(width - 1) * jnp.sqrt(i)
            weight = scale * jnp.where(eye, r + z, r) + shift
            wts[a, b] = weight
            wsend[a, b] = weight.astype(BF16)

    def w_copy(k, src, dst, dx, dy):
        return pltpu.make_async_remote_copy(
            src_ref=src, dst_ref=dst, send_sem=w_send.at[k], recv_sem=w_recv.at[k],
            device_id=at(dx, dy), device_id_type=MESH)

    def wx_copies():
        return [w_copy(0, wsend.at[na - 1], htx.at[0], 1, 0),
                w_copy(1, wsend.at[0], htx.at[1], -1, 0)]

    def wy_copies(k, first, count):
        rows = pl.ds(first, count)
        return [w_copy(k, wsend.at[rows, nbk - 1], hty.at[0, rows], 0, 1),
                w_copy(k + 1, wsend.at[rows, 0], hty.at[1, rows], 0, -1)]

    inner_wy = wy_copies(2, 2, na - 4)
    edge_wy = wy_copies(4, 0, 1) + wy_copies(6, na - 1, 1)
    last_wy = wy_copies(8, 1, 1) + wy_copies(10, na - 2, 1)
    inner = (na - 4) // 2

    def batch(i):
        h = i // inner
        r = i - inner * h
        one = (1 - h) * (2 + 2 * r) + h * r
        two = (1 - h) * (3 + 2 * r) + h * (na - 1 - r)
        return [(a, b) for a in (one, two) for b in range(nbk)]

    for k, group in enumerate(batch(0)):
        prepare(k, 0, group)
    for c in ys:
        c.wait_recv()
    total = jnp.sum(st_sum[...] + jnp.sum(st_y[...], axis=0), axis=1, keepdims=True)
    inflation = (width - 1) * total[1:2] / total[0:1]

    @pl.loop(0, inner + 1)
    def _(i):
        @pl.when(i == inner - 1)
        def _():
            for c in corner_copies():
                c.wait_recv()
            for k in range(HALO):
                for b in range(nbk + 2 * HALO):
                    grams[k, b] = landed[0, k, b]
                    grams[na + HALO + k, b] = landed[1, k, b]

        @pl.when(i == inner)
        def _():
            for c in inner_wy:
                c.start()

        transform(batch(i), i % 2, batch(i + 1))

        @pl.when(i == inner)
        def _():
            for c in wx_copies() + edge_wy:
                c.start()

    transform(batch(inner + 1), (inner + 1) % 2, [])
    for c in last_wy:
        c.start()

    def blend(a, b, lower, upper):
        left = wts[a, b - 1] if b > 0 else hty[0, a].astype(F32)
        right = wts[a, b + 1] if b < nbk - 1 else hty[1, a].astype(F32)
        out[a, b] = ((4.0 * wts[a, b] + (upper + lower) + (left + right)) * 0.125).astype(BF16)

    @pl.loop(1, na - 1)
    def _(a):
        for b in range(1, nbk - 1):
            blend(a, b, wts[a - 1, b], wts[a + 1, b])

    def row_out(a):
        return pltpu.make_async_copy(out.at[a], out_h.at[a], o_sem.at[a])

    for c in inner_wy + last_wy:
        c.wait_recv()

    @pl.loop(1, na - 1)
    def _(a):
        for b in (0, nbk - 1):
            blend(a, b, wts[a - 1, b], wts[a + 1, b])
        row_out(a).start()

    for c in edge_wy + wx_copies():
        c.wait_recv()
    for b in range(nbk):
        blend(0, b, htx[0, b].astype(F32), wts[1, b])
        blend(na - 1, b, wts[na - 2, b], htx[1, b].astype(F32))
    row_out(0).start()
    row_out(na - 1).start()
    for i in range(na // 2):
        for c in ty_copies(i):
            c.wait_send()
    for c in tx_copies() + corner_copies() + xs + ys + wx_copies() + inner_wy + edge_wy + last_wy:
        c.wait_send()
    mean_out.wait()
    for a in range(na):
        row_out(a).wait()


def apply_weights(members_h, mean_th, blended_h, out_h, members, mean_t, blended, result, sem):
    na, nbk, levels, width = members.shape
    row = lax.broadcasted_iota(jnp.int32, (width, width), 0)

    def loads(a):
        return [pltpu.make_async_copy(src.at[a], dst.at[a], sem.at[k, a])
                for k, (src, dst) in enumerate(
                    [(blended_h, blended), (mean_th, mean_t), (members_h, members)])]

    def copy_out(a):
        return pltpu.make_async_copy(result.at[a], out_h.at[a], sem.at[3, a])

    for a in range(na):
        for c in loads(a):
            c.start()

    @pl.loop(0, na)
    def _(a):
        for c in loads(a):
            c.wait()
        for b in range(nbk):
            pick = jnp.where((row == b) | (row == b + nbk) | (row == b + 2 * nbk), 1.0, 0.0)
            left = jnp.concatenate([members[a, b], mean_t[a]], axis=1)
            right = jnp.concatenate([blended[a, b], pick.astype(BF16)], axis=0)
            result[a, b] = jnp.dot(left, right, preferred_element_type=F32).astype(BF16)
        copy_out(a).start()

    @pl.loop(0, na)
    def _(a):
        copy_out(a).wait()


def shards(nx, ny, members, mean_state, obs_pert, obs_rinv, innovation, obs_count, neighbours,
           loc_weight):
    na, nbk, slots, width = obs_pert.shape
    levels = members.shape[2]
    hbm = pl.BlockSpec(memory_space=pltpu.HBM)
    dma = pltpu.SemaphoreType.DMA
    half = width // 2
    blended, mean_t = pl.pallas_call(
        functools.partial(analysis_weights, nx, ny),
        out_shape=[
            jax.ShapeDtypeStruct((na, nbk, width, width), BF16),
            jax.ShapeDtypeStruct((na, levels, width), BF16),
        ],
        in_specs=[hbm] * 7,
        out_specs=[hbm] * 2,
        scratch_shapes=[
            pltpu.VMEM((na, nbk, width, width), BF16),
            pltpu.VMEM((na, levels, width), BF16),
            pltpu.SMEM((nbk, na), jnp.int32),
            pltpu.SMEM(neighbours.shape, jnp.int32),
            pltpu.SMEM(loc_weight.shape, F32),
            pltpu.VMEM(obs_pert.shape, BF16),
            pltpu.VMEM(obs_rinv.shape, BF16),
            pltpu.VMEM(innovation.shape, BF16),
            pltpu.VMEM(mean_state.shape, F32),
            pltpu.VMEM((na + 2 * HALO, nbk + 2 * HALO, half + 16, width), BF16),
            pltpu.VMEM((2, HALO, nbk + 2 * HALO, half + 16, width), BF16),
            pltpu.VMEM((2, 2 * nbk, width, width), F32),
            pltpu.VMEM((2, 2 * nbk, 8, width), F32),
            pltpu.VMEM((na, nbk, width, width), F32),
            pltpu.VMEM((na, nbk, width, width), BF16),
            pltpu.VMEM((2, nbk, width, width), BF16),
            pltpu.VMEM((2, na, width, width), BF16),
            pltpu.VMEM((8, slots), F32),
            pltpu.VMEM((nx - 1, 8, slots), F32),
            pltpu.VMEM((8, slots), F32),
            pltpu.VMEM((ny - 1, 8, slots), F32),
            dma((7,)), dma((na // 2,)), dma((na,)),
            dma((4 + na,)), dma((4 + na,)),
            dma((nx - 1,)), dma((nx - 1,)),
            dma((ny - 1,)), dma((ny - 1,)),
            dma((12,)), dma((12,)),
        ],
        compiler_params=pltpu.CompilerParams(
            collective_id=0, has_side_effects=True, vmem_limit_bytes=57 * 1024 * 1024),
    )(obs_count.T, neighbours, loc_weight, obs_pert, obs_rinv, innovation, mean_state)
    return pl.pallas_call(
        apply_weights,
        out_shape=jax.ShapeDtypeStruct(members.shape, BF16),
        in_specs=[hbm] * 3,
        out_specs=hbm,
        scratch_shapes=[
            pltpu.VMEM(members.shape, BF16),
            pltpu.VMEM((na, levels, width), BF16),
            pltpu.VMEM((na, nbk, width, width), BF16),
            pltpu.VMEM(members.shape, BF16),
            dma((4, na)),
        ],
        compiler_params=pltpu.CompilerParams(vmem_limit_bytes=57 * 1024 * 1024),
    )(members, mean_t, blended)


def solution(mesh):
    nx, ny = mesh.shape["tx"], mesh.shape["ty"]
    return jax.shard_map(
        functools.partial(shards, nx, ny),
        mesh=mesh,
        in_specs=(
            P("tx", "ty", None, None),
            P("tx", "ty", None),
            P("tx", "ty", None, None),
            P("tx", "ty", None),
            P("tx", "ty", None),
            P("tx", "ty"),
            P("tx", "ty", None),
            P("tx", "ty", None),
        ),
        out_specs=P("tx", "ty", None, None),
        check_vma=False,
    )
```
